256 devices in a mesh: dp: 16 (over y_lo, z), blk: 16 (over y_hi, x, core).
Axes of the slice: x: 4, y: 4 (y_hi: 2, y_lo: 2; y = y_hi * 2 + y_lo), z: 8, core: 2. Of those that a mesh axis runs over, the one named last changes fastest.
Arguments:
- queries: bfloat16 [16, 2048, 512], P('dp', 'blk'), may hold values from -6 to 6
- history_keys: bfloat16 [16, 2048, 512], P('dp', 'blk'), may hold values from -6 to 6
- history_values: bfloat16 [16, 2048, 512], P('dp', 'blk'), may hold values from -6 to 6
- gate_inputs: bfloat16 [16, 2048, 512], P('dp', 'blk'), may hold values from -6 to 6
- frequencies: float32 [4, 128, 64], replicated, may hold values from -0.5 to 0.5
- out_weight: bfloat16 [512, 1024], replicated, may hold values from -0.25 to 0.25
- lengths: int32 [16, 8], P('dp'), may hold values from 1 to 1024, 2048 in all within a row
- cotangent: bfloat16 [16, 2048, 1024], P('dp', 'blk'), may hold values from -6 to 6
Outputs:
- layer_out: bfloat16 [16, 2048, 1024], P('dp', 'blk')
- grad_queries: bfloat16 [16, 2048, 512], P('dp', 'blk')
- grad_keys: bfloat16 [16, 2048, 512], P('dp', 'blk')
- grad_values: bfloat16 [16, 2048, 512], P('dp', 'blk')
- grad_gates: bfloat16 [16, 2048, 512], P('dp', 'blk')
- grad_weight: float32 [512, 1024], P('blk')
The draws below stay inside these ranges and needn't reach their ends.
Inputs may be any that keep to these rules, and one draw needn't show every extreme that they name: The 8 lengths of a row sum to 2048; in every row the longest history has exactly 1024 positions.
All inputs are finite; a program needn't handle non-finite values.
Results may differ from the reference program's by a relative error of at most 0.015.
Values may be sent and summed in bfloat16 or wider, within the bound.
No kernel may reach another device: no remote copies, remote signals or barrier semaphores. Data moves between devices by JAX's collectives and lax.ppermute only.
A program may use at most 64 MiB of HBM per device.

```python
import math
import jax
import jax.numpy as jnp
import numpy as np
from jax import lax

D = 1024
HEADS = 4
HEAD = 128
FREQS = 64
USERS = 8
TOK_DEV = 128
WIDTH = 512
SEQ = 2048
ROWS = 16
N_BLK = 16


def block_scale(stream_key, shape, cuts, low, top_value):
    gain, own = 1.0, jax.random.fold_in(stream_key, 6)
    for axis_at, blocks in cuts:
        heights = jnp.exp(jax.random.uniform(jax.random.fold_in(own, axis_at), (blocks,), jnp.float32, low / len(cuts), top_value / len(cuts)))
        gain = gain * jnp.repeat(heights, shape[axis_at] // blocks).reshape([-1 if axis == axis_at else 1 for axis in range(len(shape))])
    return gain


def split_up(number_of, total, limit, slope):
    weights = [(1 << 20) // math.isqrt(grade ** slope) + 1 for grade in range(2, number_of + 1)]
    surplus, given = total - limit - (number_of - 1), [1] * (number_of - 1)
    while surplus > 0:
        candidates = [i for i in range(number_of - 1) if given[i] < limit]
        mass, budget = sum([weights[i] for i in candidates]), surplus
        for i in candidates:
            addition = min(limit - given[i], max(1, budget * weights[i] // mass), surplus)
            given[i] = given[i] + addition
            surplus = surplus - addition
    return np.array([limit] + given)


def ragged(stream_key, number_of, total, bound, slope):
    if number_of == 2:
        one = jax.random.randint(stream_key, (), max(1, total - bound), min(bound, total - 1) + 1)
        return jnp.stack([one, total - one])
    sizes = jnp.asarray(split_up(number_of, total, bound, slope), jnp.int32)
    pairs = (number_of - 1) // 2
    source_of, sink = sizes[1:1 + 2 * pairs:2], sizes[2:2 + 2 * pairs:2]
    margin = jnp.minimum(source_of - 1, bound - sink)
    passed = jax.random.randint(jax.random.fold_in(stream_key, 1), (pairs,), 0, 1 << 20) % (margin + 1)
    sizes = sizes.at[1:1 + 2 * pairs:2].set(source_of - passed).at[2:2 + 2 * pairs:2].set(sink + passed)
    return sizes[jax.random.permutation(jax.random.fold_in(stream_key, 2), number_of)]


def bell_draw(own_key, shape, width, most, pieces=(), held_as=jnp.bfloat16):
    gain = block_scale(own_key, shape, pieces, -0.22, 0.18) if pieces else 1.0
    values = jax.random.normal(own_key, shape, jnp.float32) * width * gain
    return jnp.minimum(jnp.maximum(values, -most), most).astype(held_as)


def setup_inputs(seed: int = 0) -> dict:
    keys = jax.random.split(jax.random.key(seed), 9)
    queries = bell_draw(keys[0], (ROWS, SEQ, WIDTH), 1.0, 6.0, ((0, 16), (1, 16)))
    history_keys = bell_draw(keys[1], (ROWS, SEQ, WIDTH), 1.0, 6.0, ((0, 16), (1, 16)))
    history_values = bell_draw(keys[2], (ROWS, SEQ, WIDTH), 1.0, 6.0, ((0, 16), (1, 16)))
    gate_inputs = bell_draw(keys[3], (ROWS, SEQ, WIDTH), 1.0, 6.0, ((0, 16), (1, 16)))
    frequencies = bell_draw(keys[4], (HEADS, HEAD, FREQS), HEAD ** -0.5, 0.5, (), jnp.float32)
    out_weight = bell_draw(keys[5], (WIDTH, D), WIDTH ** -0.5, 0.25)
    lengths = jax.vmap(lambda own: ragged(own, USERS, SEQ, SEQ // 2, 2))(jax.random.split(keys[6], ROWS)).reshape((ROWS, USERS)).astype(jnp.int32)
    cotangent = bell_draw(keys[7], (ROWS, SEQ, D), 1.0, 6.0, ((0, 16), (1, 16)))
    return {"queries": queries, "history_keys": history_keys, "history_values": history_values, "gate_inputs": gate_inputs, "frequencies": frequencies, "out_weight": out_weight, "lengths": lengths, "cotangent": cotangent}


EPS = 1e-05
HIGHEST_PRECISION = lax.Precision.HIGHEST

def user_index(positions, user_ends):
    return lax.optimization_barrier(jnp.sum((positions[:, None] >= user_ends[None, :]).astype(jnp.int32), axis=1, dtype=jnp.int32))

def user_layout(lengths_row, positions):
    user_ends = jnp.cumsum(lengths_row, dtype=jnp.int32)
    user_starts = user_ends - lengths_row
    user_ids = user_index(positions, user_ends)
    picked = (user_ids[:, None] == jnp.arange(lengths_row.shape[0], dtype=jnp.int32)[None, :]).astype(jnp.int32)
    first_pos = lax.optimization_barrier(jnp.sum(picked * user_starts[None, :], axis=1, dtype=jnp.int32))
    return (user_ids, positions - first_pos + 1)

def feature_map(angles):
    return (jnp.concatenate([jnp.cos(angles), jnp.sin(angles)], axis=-1) / math.sqrt(FREQS)).astype(jnp.bfloat16)

def feature_grad(angles, grad_phi, frequencies):
    grad_angles = (jnp.cos(angles) * grad_phi[..., FREQS:] - jnp.sin(angles) * grad_phi[..., :FREQS]) / math.sqrt(FREQS)
    return jnp.einsum('thf,hdf->thd', grad_angles, frequencies, precision=HIGHEST_PRECISION)

def silu_slope(scores):
    sigma = jax.nn.sigmoid(scores)
    return sigma * (1.0 + scores * (1.0 - sigma))

def one_row(queries, keys_row, values_row, gates_row, frequencies, out_weight, lengths_row, cotangent):
    score_scale = 1.0 / math.sqrt(HEAD)
    positions = jnp.arange(SEQ, dtype=jnp.int32)
    user_ids, counts = user_layout(lengths_row, positions)
    key_heads = keys_row.reshape(SEQ, HEADS, HEAD).astype(jnp.float32)
    value_heads = values_row.reshape(SEQ, HEADS, HEAD).astype(jnp.float32)
    key_angles = jnp.einsum('shd,hdf->shf', key_heads, frequencies, precision=HIGHEST_PRECISION)
    key_phi = feature_map(key_angles).astype(jnp.float32)

    def block_step(carry, inputs):
        key_attn, value_attn, grad_kphi, value_recall, grad_weight = carry
        query_blk, gate_blk, cot_blk, query_pos = inputs
        query_users = user_ids[query_pos]
        query_counts = counts[query_pos].astype(jnp.float32)
        rows = query_blk.shape[0]
        query_heads = query_blk.reshape(rows, HEADS, HEAD).astype(jnp.float32)
        allowed = ((positions[None, :] <= query_pos[:, None]) & (user_ids[None, :] == query_users[:, None])).astype(jnp.float32)
        scores = jnp.einsum('thd,shd->hts', query_heads, key_heads, precision=HIGHEST_PRECISION) * score_scale
        weights = (jax.nn.silu(scores) * allowed).astype(jnp.bfloat16)
        attended = jnp.einsum('hts,shd->thd', weights.astype(jnp.float32), value_heads, precision=HIGHEST_PRECISION)
        query_angles = jnp.einsum('thd,hdf->thf', query_heads, frequencies, precision=HIGHEST_PRECISION)
        query_phi = feature_map(query_angles).astype(jnp.float32)
        kernel = jnp.einsum('thf,shf->hts', query_phi, key_phi, precision=HIGHEST_PRECISION) * allowed
        recalled = jnp.einsum('hts,shd->thd', kernel, value_heads, precision=HIGHEST_PRECISION)
        gate_float = gate_blk.astype(jnp.float32)
        gate = jax.nn.sigmoid(lax.optimization_barrier(jnp.sum(gate_float.reshape(rows, HEADS, HEAD), axis=-1)) * score_scale)
        mixed = ((attended + gate[..., None] * recalled) / query_counts[:, None, None]).reshape(rows, WIDTH)
        centered = mixed - lax.optimization_barrier(jnp.mean(mixed, axis=1, keepdims=True))
        rstd = lax.rsqrt(lax.optimization_barrier(jnp.mean(centered * centered, axis=1, keepdims=True)) + EPS)
        normed = centered * rstd
        hidden = (normed * gate_float).astype(jnp.bfloat16)
        out_blk = jnp.dot(hidden, out_weight, preferred_element_type=jnp.float32).astype(jnp.bfloat16)
        grad_hidden = jnp.dot(cot_blk, out_weight.T, preferred_element_type=jnp.float32)
        grad_weight = grad_weight + jnp.dot(hidden.T, cot_blk, preferred_element_type=jnp.float32)
        grad_normed = grad_hidden * gate_float
        grad_mixed = rstd * (grad_normed - lax.optimization_barrier(jnp.mean(grad_normed, axis=1, keepdims=True)) - normed * lax.optimization_barrier(jnp.mean(grad_normed * normed, axis=1, keepdims=True)))
        scaled = (grad_mixed / query_counts[:, None]).reshape(rows, HEADS, HEAD)
        scaled_b = scaled.astype(jnp.bfloat16).astype(jnp.float32)
        gate_term = lax.optimization_barrier(jnp.sum(scaled * recalled, axis=-1)) * gate * (1.0 - gate) * score_scale
        grad_gate = grad_hidden * normed + jnp.broadcast_to(gate_term[..., None], (rows, HEADS, HEAD)).reshape(rows, WIDTH)
        value_part = jnp.einsum('hts,thd->shd', weights.astype(jnp.float32), scaled_b, precision=HIGHEST_PRECISION)
        grad_w = jnp.einsum('thd,shd->hts', scaled_b, value_heads, precision=HIGHEST_PRECISION)
        grad_scores = (grad_w * silu_slope(scores) * allowed * score_scale).astype(jnp.bfloat16).astype(jnp.float32)
        grad_q = jnp.einsum('hts,shd->thd', grad_scores, key_heads, precision=HIGHEST_PRECISION)
        key_part = jnp.einsum('hts,thd->shd', grad_scores, query_heads, precision=HIGHEST_PRECISION)
        key_attn = key_attn + lax.optimization_barrier(key_part.astype(jnp.bfloat16)).astype(jnp.float32)
        value_attn = value_attn + lax.optimization_barrier(value_part.astype(jnp.bfloat16)).astype(jnp.float32)
        grad_recall = gate[..., None] * scaled
        grad_kernel = jnp.einsum('thd,shd->hts', grad_recall, value_heads, precision=HIGHEST_PRECISION) * allowed
        value_recall = value_recall + jnp.einsum('hts,thd->shd', kernel, grad_recall, precision=HIGHEST_PRECISION)
        grad_qphi = jnp.einsum('hts,shf->thf', grad_kernel, key_phi, precision=HIGHEST_PRECISION)
        grad_kphi = grad_kphi + jnp.einsum('hts,thf->shf', grad_kernel, query_phi, precision=HIGHEST_PRECISION)
        grad_q = grad_q + feature_grad(query_angles, grad_qphi, frequencies)
        outputs = (out_blk, grad_q.reshape(rows, WIDTH).astype(jnp.bfloat16), grad_gate.astype(jnp.bfloat16))
        return ((key_attn, value_attn, grad_kphi, value_recall, grad_weight), outputs)
    zero_heads = jnp.zeros((SEQ, HEADS, HEAD), jnp.float32)
    init = (zero_heads, zero_heads, jnp.zeros((SEQ, HEADS, 2 * FREQS), jnp.float32), zero_heads, jnp.zeros((WIDTH, D), jnp.float32))
    inputs = (queries.reshape(N_BLK, TOK_DEV, WIDTH), gates_row.reshape(N_BLK, TOK_DEV, WIDTH), cotangent.reshape(N_BLK, TOK_DEV, D), positions.reshape(N_BLK, TOK_DEV))
    carry, outputs = lax.scan(block_step, init, inputs)
    key_attn, value_attn, grad_kphi, value_recall, grad_weight = carry
    out_row = outputs[0].reshape(SEQ, D)
    grad_queries = outputs[1].reshape(SEQ, WIDTH)
    grad_gates = outputs[2].reshape(SEQ, WIDTH)
    grad_keys = (key_attn + feature_grad(key_angles, grad_kphi, frequencies)).reshape(SEQ, WIDTH).astype(jnp.bfloat16)
    grad_values = (value_attn + value_recall).reshape(SEQ, WIDTH).astype(jnp.bfloat16)
    return (out_row, grad_queries, grad_keys, grad_values, grad_gates, grad_weight)

def reference(queries, history_keys, history_values, gate_inputs, frequencies, out_weight, lengths, cotangent):

    def row_step(total, inputs):
        query_row, key_row, value_row, gate_row, lengths_row, cot_row = inputs
        result = one_row(query_row, key_row, value_row, gate_row, frequencies, out_weight, lengths_row, cot_row)
        return (total + result[5], result[:5])
    total, stacked = lax.scan(row_step, jnp.zeros((WIDTH, D), jnp.float32), (queries, history_keys, history_values, gate_inputs, lengths, cotangent))
    return (stacked[0], stacked[1], stacked[2], stacked[3], stacked[4], total)
```

```python
import functools
import math

import jax
import jax.numpy as jnp
from jax import lax
from jax.experimental import pallas as pl
from jax.experimental.pallas import tpu as pltpu
from jax.sharding import PartitionSpec as P

EPS = 1e-05
HEADS, HEAD, FREQS, USERS = 4, 128, 64, 8
TOK, NBLK, GROUPS = 128, 16, 4
SUB = TOK // GROUPS
WIDTH, D = HEADS * HEAD, 1024
SEQ = TOK * NBLK
QROWS = SUB * NBLK
TILE = 2 * TOK
STEP = 2 * SUB
REACH = 5
TILES = SEQ // TILE
SCALE = 1.0 / math.sqrt(HEAD)
F32, BF16 = jnp.float32, jnp.bfloat16

Q0, G0, K0, V0, PACK = 0, SUB, 2 * SUB, 2 * SUB + TOK, 2 * SUB + 2 * TOK
WROWS = (WIDTH // NBLK) * D // HEAD

NT = (((1,), (1,)), ((), ()))
NN = (((1,), (0,)), ((), ()))
TN = (((0,), (0,)), ((), ()))


def mm(a, b, dims):
    return lax.dot_general(a, b, dims, preferred_element_type=F32)


def lanes(shape):
    return lax.broadcasted_iota(jnp.int32, shape, 1)


def starts_of(lens_ref, pos):
    end = jnp.int32(0)
    start = jnp.zeros_like(pos)
    for u in range(USERS):
        end = end + lens_ref[u]
        start = jnp.where(pos >= end, end, start)
    return start


def cos_sin(angles):
    turns = jnp.floor(angles * (2.0 / math.pi) + 0.5)
    r = angles - turns * 1.5703125
    r = r - turns * 4.837512969970703125e-4
    r = r - turns * 7.54978995489188e-8
    quad = turns.astype(jnp.int32) - jnp.where(lanes(angles.shape) >= FREQS, 1, 0)
    z = r * r
    c = 1.0 - 0.5 * z + z * z * (4.166664568e-2 + z * (-1.388731625e-3 + z * 2.443315712e-5))
    s = r + r * z * (-1.6666654611e-1 + z * (8.3321608736e-3 - z * 1.9515295891e-4))
    odd = (quad & 1) == 1
    value = jnp.where(odd, s, c)
    return jnp.where(((quad + 1) & 2) == 2, -value, value)


def pack_kernel(q_ref, k_ref, v_ref, u_ref, out_ref):
    for h in range(HEADS):
        cols = slice(h * HEAD, (h + 1) * HEAD)
        total = jnp.sum(u_ref[:, cols].astype(F32), axis=1, keepdims=True)
        gate = jnp.broadcast_to(jax.nn.sigmoid(total * SCALE), (TOK, HEAD))
        high = gate.astype(BF16).astype(F32)
        gate = jnp.where(lanes((TOK, HEAD)) < FREQS, high, gate - high).astype(BF16)
        keys, values = k_ref[:, cols], v_ref[:, cols]
        for g in range(GROUPS):
            rows = slice(g * SUB, (g + 1) * SUB)
            out_ref[h * GROUPS + g, Q0:G0, :] = q_ref[rows, cols]
            out_ref[h * GROUPS + g, G0:K0, :] = gate[rows]
            out_ref[h * GROUPS + g, K0:V0, :] = keys
            out_ref[h * GROUPS + g, V0:PACK, :] = values


def stage_rows(recv_ref, lens_ref, group, q_s, gate_s, start_s, pos_s):
    for b in range(NBLK):
        rows = slice(b * SUB, (b + 1) * SUB)
        q_s[rows, :] = recv_ref[b, Q0:G0, :]
        parts = recv_ref[b, G0:K0, :].astype(F32)
        gate_s[rows, :] = jnp.broadcast_to(
            parts[:, 0:1] + parts[:, FREQS : FREQS + 1], (SUB, HEAD)
        )
    row = lax.broadcasted_iota(jnp.int32, (QROWS, HEAD), 0)
    pos = (row >> 5) * TOK + group * SUB + (row & (SUB - 1))
    pos_s[...] = pos
    start_s[...] = starts_of(lens_ref, pos)


def tile_of(recv_ref, c, first, last):
    return jnp.concatenate(
        [recv_ref[2 * c, first:last, :], recv_ref[2 * c + 1, first:last, :]], axis=0
    )


def twice(a):
    return jnp.concatenate([a, a], axis=1)


def allowed_of(start_s, pos_s, rows, c):
    key = c * TILE + lanes((rows.stop - rows.start, TILE))
    return (key >= twice(start_s[rows, :])) & (key <= twice(pos_s[rows, :]))


def forward_kernel(
    lens_ref, idx_ref, recv_ref, freq_ref, mixed_ref, phiq_ref, phik_ref,
    q_s, gate_s, start_s, pos_s, acc_s,
):
    head, group = idx_ref[0] // GROUPS, idx_ref[0] % GROUPS
    stage_rows(recv_ref, lens_ref, group, q_s, gate_s, start_s, pos_s)
    freq = freq_ref[head]
    freq = jnp.concatenate([freq, freq], axis=1)
    pieces = []
    for _ in range(3):
        piece = freq.astype(BF16)
        pieces.append(piece)
        freq = freq - piece.astype(F32)
    pieces = jnp.concatenate(pieces, axis=1)

    def phi_of(x):
        a = mm(x, pieces, NN)
        angles = (a[:, 2 * HEAD :] + a[:, HEAD : 2 * HEAD]) + a[:, :HEAD]
        return (cos_sin(angles) / math.sqrt(FREQS)).astype(BF16)

    for i in range(QROWS // TILE):
        rows = slice(i * TILE, (i + 1) * TILE)
        phiq_ref[rows, :] = phi_of(q_s[rows, :])
    acc_s[...] = jnp.zeros_like(acc_s)
    for c in range(TILES):
        rows = slice(c * STEP, min(c + REACH, TILES) * STEP)
        keys = tile_of(recv_ref, c, K0, V0)
        values = tile_of(recv_ref, c, V0, PACK)
        phik = phi_of(keys)
        phik_ref[c * TILE : (c + 1) * TILE, :] = phik
        half = mm(q_s[rows, :], keys, NT) * (0.5 * SCALE)
        weights = half + half * jnp.tanh(half)
        kern = mm(phiq_ref[rows, :], phik, NT)
        both = weights + twice(gate_s[rows, :]) * kern
        both = jnp.where(allowed_of(start_s, pos_s, rows, c), both, 0.0).astype(BF16)
        acc_s[rows, :] += mm(both, values, NN)
    for b in range(NBLK):
        rows = slice(b * SUB, (b + 1) * SUB)
        count = (pos_s[rows, :] - start_s[rows, :] + 1).astype(F32)
        mixed_ref[b] = acc_s[rows, :] / count


def middle_kernel(
    lens_ref, idx_ref, mixed_ref, u_ref, w_ref, cot_ref, out_ref, send_ref, ghn_ref, hid_s
):
    pos = idx_ref[0] * TOK + lax.broadcasted_iota(jnp.int32, (TOK, HEAD), 0)
    count = (pos - starts_of(lens_ref, pos) + 1).astype(F32)
    count = jnp.concatenate([count] * HEADS, axis=1)
    mixed = jnp.concatenate(
        [
            jnp.concatenate([mixed_ref[h * GROUPS + g] for g in range(GROUPS)], axis=0)
            for h in range(HEADS)
        ],
        axis=1,
    )
    gates = u_ref[...].astype(F32)
    centered = mixed - jnp.mean(mixed, axis=1, keepdims=True)
    rstd = lax.rsqrt(jnp.mean(centered * centered, axis=1, keepdims=True) + EPS)
    normed = centered * rstd
    hidden = (normed * gates).astype(BF16)
    hid_s[...] = hidden
    out_ref[...] = mm(hidden, w_ref[...], NN).astype(BF16)
    grad_hidden = mm(cot_ref[...], w_ref[...], NT)
    ghn_ref[...] = grad_hidden * normed
    grad_normed = grad_hidden * gates
    grad_mixed = rstd * (
        grad_normed
        - jnp.mean(grad_normed, axis=1, keepdims=True)
        - normed * jnp.mean(grad_normed * normed, axis=1, keepdims=True)
    )
    scaled = (grad_mixed / count).astype(BF16)
    for h in range(HEADS):
        for g in range(GROUPS):
            send_ref[h * GROUPS + g, 0:SUB, :] = scaled[
                g * SUB : (g + 1) * SUB, h * HEAD : (h + 1) * HEAD
            ]
    for j in range(D // HEAD):
        part = mm(hid_s[...], cot_ref[:, j * HEAD : (j + 1) * HEAD], TN).astype(BF16)
        for d in range(NBLK):
            send_ref[d, SUB + j * 32 : SUB + (j + 1) * 32, :] = part[d * 32 : (d + 1) * 32]


def backward_kernel(
    lens_ref, idx_ref, recv_ref, phiq_ref, phik_ref, grads_ref, freq_ref, send_ref, gw_ref,
    q_s, gate_s, start_s, pos_s, sc_s, dq_s, dphi_s, term_s,
):
    head, group = idx_ref[0] // GROUPS, idx_ref[0] % GROUPS
    stage_rows(recv_ref, lens_ref, group, q_s, gate_s, start_s, pos_s)
    total = grads_ref[0, SUB:, :].astype(F32)
    for d in range(1, NBLK):
        total = total + grads_ref[d, SUB:, :].astype(F32)
    piece = WROWS // NBLK
    for d in range(NBLK):
        gw_ref[d] = total[d * piece : (d + 1) * piece].astype(BF16)
    for b in range(NBLK):
        sc_s[b * SUB : (b + 1) * SUB, :] = grads_ref[b, 0:SUB, :]
    freq = freq_ref[head].astype(BF16)
    freq = jnp.concatenate([freq, -freq], axis=1)
    dq_s[...] = jnp.zeros_like(dq_s)
    dphi_s[...] = jnp.zeros_like(dphi_s)
    term_s[...] = jnp.zeros_like(term_s)

    def back(phi, grad_phi):
        turned = pltpu.roll(grad_phi, FREQS, 1)
        return mm((phi.astype(F32) * turned).astype(BF16), freq, NT)

    for c in range(TILES):
        rows = slice(c * STEP, min(c + REACH, TILES) * STEP)
        keys = tile_of(recv_ref, c, K0, V0)
        values = tile_of(recv_ref, c, V0, PACK)
        phik = phik_ref[c * TILE : (c + 1) * TILE, :]
        q, phiq, scaled = q_s[rows, :], phiq_ref[rows, :], sc_s[rows, :]
        gate = twice(gate_s[rows, :])
        allowed = allowed_of(start_s, pos_s, rows, c)
        half = mm(q, keys, NT) * (0.5 * SCALE)
        t = jnp.tanh(half)
        weights = half + half * t
        slope = (1.0 + t) + weights * (1.0 - t)
        kern = mm(phiq, phik, NT)
        grad_w = jnp.where(allowed, mm(scaled, values, NT), 0.0)
        both = jnp.where(allowed, weights + gate * kern, 0.0).astype(BF16)
        grad_s = (grad_w * slope * (0.5 * SCALE)).astype(BF16)
        grad_k = (grad_w * gate).astype(BF16)
        term = kern * grad_w
        term_s[rows, :] += term[:, :TOK] + term[:, TOK:]
        dq_s[rows, :] += mm(grad_s, keys, NN)
        dphi_s[rows, :] += mm(grad_k, phik, NN)
        dkey = mm(grad_s, q, TN) + back(phik, mm(grad_k, phiq, TN))
        dval = mm(both, scaled, TN)
        for i in range(2):
            send_ref[2 * c + i, K0:V0, :] = dkey[i * TOK : (i + 1) * TOK].astype(BF16)
            send_ref[2 * c + i, V0:PACK, :] = dval[i * TOK : (i + 1) * TOK].astype(BF16)
    dq = dq_s[...] + back(phiq_ref[...], dphi_s[...])
    gate = gate_s[...]
    term = jnp.sum(term_s[...], axis=1, keepdims=True) * gate * (1.0 - gate) * SCALE
    for b in range(NBLK):
        rows = slice(b * SUB, (b + 1) * SUB)
        send_ref[b, Q0:G0, :] = dq[rows].astype(BF16)
        send_ref[b, G0:K0, :] = term[rows].astype(BF16)


def final_kernel(recv_ref, ghn_ref, gw_ref, dq_ref, dk_ref, dv_ref, dg_ref, dw_ref):
    for h in range(HEADS):
        cols = slice(h * HEAD, (h + 1) * HEAD)
        keys = values = 0.0
        for g in range(GROUPS):
            rows = slice(g * SUB, (g + 1) * SUB)
            d = h * GROUPS + g
            dq_ref[rows, cols] = recv_ref[d, Q0:G0, :]
            dg_ref[rows, cols] = (ghn_ref[rows, cols] + recv_ref[d, G0:K0, :].astype(F32)).astype(
                BF16
            )
            keys = keys + recv_ref[d, K0:V0, :].astype(F32)
            values = values + recv_ref[d, V0:PACK, :].astype(F32)
        dk_ref[:, cols] = keys.astype(BF16)
        dv_ref[:, cols] = values.astype(BF16)
    share = WIDTH // NBLK
    for j in range(D // HEAD):
        for i in range(2):
            rows = gw_ref[2 * j + i].astype(F32)
            dw_ref[i * 16 : (i + 1) * 16, j * HEAD : (j + 1) * HEAD] = rows


VMEM = pl.BlockSpec(memory_space=pltpu.VMEM)
SMEM = pl.BlockSpec(memory_space=pltpu.SMEM)


def call(body, scalars, arrays, outs, scratch=()):
    return pl.pallas_call(
        body,
        in_specs=[SMEM] * len(scalars) + [VMEM] * len(arrays),
        out_specs=[VMEM] * len(outs),
        out_shape=[jax.ShapeDtypeStruct(s, t) for s, t in outs],
        scratch_shapes=[pltpu.VMEM(s, t) for s, t in scratch],
        compiler_params=pltpu.CompilerParams(vmem_limit_bytes=40 * 1024 * 1024),
    )(*scalars, *arrays)


def swap(a, axis):
    return lax.all_to_all(a, axis, 0, 0, tiled=True)


def local(q, k, v, u, freqs, w, lens, cot):
    q, k, v, u, cot, lens = q[0], k[0], v[0], u[0], cot[0], lens[0]
    idx = lax.axis_index("blk").astype(jnp.int32)[None]
    staged = [
        ((QROWS, HEAD), BF16),
        ((QROWS, HEAD), F32),
        ((QROWS, HEAD), jnp.int32),
        ((QROWS, HEAD), jnp.int32),
    ]
    (send1,) = call(pack_kernel, [], [q, k, v, u], [((NBLK, PACK, HEAD), BF16)])
    recv1 = swap(send1, "blk")
    mixed, phiq, phik = call(
        forward_kernel,
        [lens, idx],
        [recv1, freqs],
        [((NBLK, SUB, HEAD), F32), ((QROWS, HEAD), BF16), ((SEQ, HEAD), BF16)],
        staged + [((QROWS, HEAD), F32)],
    )
    recv2 = swap(mixed, "blk")
    layer_out, send3, ghn = call(
        middle_kernel,
        [lens, idx],
        [recv2, u, w, cot],
        [((TOK, D), BF16), ((NBLK, SUB + WROWS, HEAD), BF16), ((TOK, WIDTH), F32)],
        [((TOK, WIDTH), BF16)],
    )
    recv3 = swap(send3, "blk")
    send4, gw = call(
        backward_kernel,
        [lens, idx],
        [recv1, phiq, phik, recv3, freqs],
        [((NBLK, PACK, HEAD), BF16), ((NBLK, WROWS // NBLK, HEAD), BF16)],
        staged + [((QROWS, HEAD), BF16)] + [((QROWS, HEAD), F32)] * 3,
    )
    recv4 = swap(send4, "blk")
    parts = swap(gw, "dp")
    mine = jnp.sum(parts.astype(F32), axis=0).astype(BF16)
    whole = swap(jnp.broadcast_to(mine[None], gw.shape), "dp")
    dq, dk, dv, dg, dw = call(
        final_kernel,
        [],
        [recv4, ghn, whole],
        [((TOK, WIDTH), BF16)] * 4 + [((WIDTH // NBLK, D), F32)],
    )
    return layer_out[None], dq[None], dk[None], dv[None], dg[None], dw


def solution(mesh):
    rows = P("dp", "blk", None)
    return jax.shard_map(
        local,
        mesh=mesh,
        in_specs=(rows, rows, rows, rows, P(), P(), P("dp", None), rows),
        out_specs=(rows, rows, rows, rows, rows, P("blk", None)),
        check_vma=False,
    )
```

```python
import functools
import math

import jax
import jax.numpy as jnp
from jax import lax
from jax.experimental import pallas as pl
from jax.experimental.pallas import tpu as pltpu
from jax.sharding import PartitionSpec as P

EPS = 1e-05
HEADS, HEAD, FREQS, USERS = 4, 128, 64, 8
TOK, NBLK = 128, 16
SUB = TOK // 2
WIDTH, D = HEADS * HEAD, 1024
ROWS = SUB * NBLK
TILE = 2 * SUB
REACH = 5
TILES = ROWS // TILE
SCALE = 1.0 / math.sqrt(HEAD)
F32, BF16 = jnp.float32, jnp.bfloat16

Q0, G0, K0, V0, PACK = 0, SUB, SUB + 16, 2 * SUB + 16, 3 * SUB + 16
WROWS = (WIDTH // NBLK) * D // HEAD


def device(h, gq, gk):
    return 4 * h + 2 * gq + gk


NT = (((1,), (1,)), ((), ()))
NN = (((1,), (0,)), ((), ()))
TN = (((0,), (0,)), ((), ()))


def mm(a, b, dims):
    return lax.dot_general(a, b, dims, preferred_element_type=F32)


def lanes(shape):
    return lax.broadcasted_iota(jnp.int32, shape, 1)


def sublanes(shape):
    return lax.broadcasted_iota(jnp.int32, shape, 0)


def column(row, mine):
    return jnp.sum(jnp.where(mine, row, 0.0), axis=1, keepdims=True)


def starts_of(lens_ref, pos):
    end = jnp.int32(0)
    start = jnp.zeros_like(pos)
    for u in range(USERS):
        end = end + lens_ref[u]
        start = jnp.where(pos >= end, end, start)
    return start


def cos_sin(angles):
    turns = jnp.floor(angles * (2.0 / math.pi) + 0.5)
    r = angles - turns * 1.5703125
    r = r - turns * 4.837512969970703125e-4
    r = r - turns * 7.54978995489188e-8
    quad = turns.astype(jnp.int32) - jnp.where(lanes(angles.shape) >= FREQS, 1, 0)
    z = r * r
    c = 1.0 - 0.5 * z + z * z * (4.166664568e-2 + z * (-1.388731625e-3 + z * 2.443315712e-5))
    s = r + r * z * (-1.6666654611e-1 + z * (8.3321608736e-3 - z * 1.9515295891e-4))
    odd = (quad & 1) == 1
    value = jnp.where(odd, s, c)
    return jnp.where(((quad + 1) & 2) == 2, -value, value)


def pack_kernel(q_hbm, k_hbm, v_hbm, u_hbm, out_ref, q_ref, k_ref, v_ref, u_ref, sems):
    pairs = ((u_hbm, u_ref), (q_hbm, q_ref), (k_hbm, k_ref), (v_hbm, v_ref))
    copies = [pltpu.make_async_copy(src, dst, sems.at[i]) for i, (src, dst) in enumerate(pairs)]
    for copy in copies:
        copy.start()
    ones = jnp.ones((16, HEAD), BF16)
    copies[0].wait()
    for h in range(HEADS):
        total = mm(ones, u_ref[:, h * HEAD : (h + 1) * HEAD], NT)
        gate = jax.nn.sigmoid(total * SCALE)
        high = gate.astype(BF16).astype(F32)
        gate = jnp.where(sublanes((16, TOK)) < 8, high, gate - high).astype(BF16)
        for d in range(device(h, 0, 0), device(h, 1, 1) + 1):
            out_ref[d, G0:K0, :] = gate
    for copy in copies[1:]:
        copy.wait()
    for h in range(HEADS):
        cols = slice(h * HEAD, (h + 1) * HEAD)
        for gq in range(2):
            for gk in range(2):
                d = device(h, gq, gk)
                out_ref[d, Q0:G0, :] = q_ref[gq * SUB : (gq + 1) * SUB, cols]
                out_ref[d, K0:V0, :] = k_ref[gk * SUB : (gk + 1) * SUB, cols]
                out_ref[d, V0:PACK, :] = v_ref[gk * SUB : (gk + 1) * SUB, cols]


def stage_rows(recv_ref, lens_ref, gq, qp_s, gate_s, start_s, pos_s):
    pos = sublanes((NBLK, TOK)) * TOK + lanes((NBLK, TOK))
    starts = starts_of(lens_ref, pos).astype(F32)
    first = (sublanes((SUB, HEAD)) + gq * SUB).astype(F32)
    mine = lanes((SUB, TOK)) == sublanes((SUB, TOK)) + gq * SUB
    for b in range(NBLK):
        rows = slice(b * SUB, (b + 1) * SUB)
        qp_s[rows, :HEAD] = recv_ref[b, Q0:G0, :]
        parts = recv_ref[b, G0:K0, :].astype(F32)
        gate_s[rows, :] = jnp.broadcast_to(column(parts[0:1] + parts[8:9], mine), (SUB, HEAD))
        start_s[rows, :] = jnp.broadcast_to(column(starts[b : b + 1], mine), (SUB, HEAD))
        pos_s[rows, :] = first + float(b * TOK)


def tile_of(recv_ref, c, first, last):
    return jnp.concatenate(
        [recv_ref[2 * c, first:last, :], recv_ref[2 * c + 1, first:last, :]], axis=0
    )


def diagonal(a, b):
    zero = jnp.zeros_like(a)
    return jnp.concatenate(
        [jnp.concatenate([a, zero], axis=1), jnp.concatenate([zero, b], axis=1)], axis=0
    )


def masker(start_s, pos_s, rows, c, gk):
    lane = lanes((1, TILE))
    key = ((2 * c + (lane >> 6)) * TOK + gk * SUB + (lane & (SUB - 1))).astype(F32)
    top = slice(rows.start, rows.start + TILE)
    near = (key >= start_s[top, :]) & (key <= pos_s[top, :])
    if rows.stop == top.stop:
        return lambda x: jnp.where(near, x, 0.0)
    far = key >= start_s[top.stop : rows.stop, :]

    def masked(x):
        return jnp.concatenate(
            [jnp.where(near, x[:TILE], 0.0), jnp.where(far, x[TILE:], 0.0)], axis=0
        )

    return masked


def place(idx_ref):
    return idx_ref[0] // 4, (idx_ref[0] // 2) % 2, idx_ref[0] % 2


def tile_rows(c):
    return slice(c * TILE, min(c + REACH, TILES) * TILE)


def forward_kernel(
    lens_ref, idx_ref, recv_ref, freq_ref, mixed_ref, phiq_ref, phik_ref,
    qp_s, gate_s, start_s, pos_s, acc_s,
):
    head, gq, gk = place(idx_ref)
    stage_rows(recv_ref, lens_ref, gq, qp_s, gate_s, start_s, pos_s)
    freq = freq_ref[head]
    freq = jnp.concatenate([freq, freq], axis=1)
    pieces = []
    for _ in range(3):
        piece = freq.astype(BF16)
        pieces.append(piece)
        freq = freq - piece.astype(F32)
    pieces = jnp.concatenate(pieces, axis=1)

    def phi_of(x):
        a = mm(x, pieces, NN)
        angles = (a[:, 2 * HEAD :] + a[:, HEAD : 2 * HEAD]) + a[:, :HEAD]
        return (cos_sin(angles) / math.sqrt(FREQS)).astype(BF16)

    for i in range(4):
        rows = slice(i * ROWS // 4, (i + 1) * ROWS // 4)
        phiq = phi_of(qp_s[rows, :HEAD])
        phiq_ref[rows, :] = phiq
        qp_s[rows, HEAD:] = phiq
    acc_s[...] = jnp.zeros_like(acc_s)
    for c in range(TILES):
        rows = tile_rows(c)
        keys = tile_of(recv_ref, c, K0, V0)
        values = tile_of(recv_ref, c, V0, PACK)
        phik = phi_of(keys)
        phik_ref[c * TILE : (c + 1) * TILE, :] = phik
        both = mm(qp_s[rows, :], diagonal(keys, phik), NT)
        half, kern = both[:, :TILE] * (0.5 * SCALE), both[:, TILE:]
        both = half + half * jnp.tanh(half) + gate_s[rows, :] * kern
        both = masker(start_s, pos_s, rows, c, gk)(both).astype(BF16)
        acc_s[rows, :] += mm(both, values, NN)
    for b in range(NBLK):
        mixed_ref[b] = acc_s[b * SUB : (b + 1) * SUB, :].astype(BF16)


def hidden_grad_kernel(w_ref, cot_ref, gh_ref):
    gh_ref[...] = mm(cot_ref[...], w_ref[...], NT)


def middle_kernel(
    lens_ref, idx_ref, mixed_ref, u_ref, gh_ref, cot_ref, hid_ref, send_ref, ghn_ref
):
    pos = idx_ref[0] * TOK + sublanes((TOK, HEAD))
    count = (pos - starts_of(lens_ref, pos) + 1).astype(F32)
    inverse = jnp.concatenate([1.0 / count] * HEADS, axis=1)
    mixed = []
    for h in range(HEADS):
        halves = [
            mixed_ref[device(h, gq, 0)].astype(F32) + mixed_ref[device(h, gq, 1)].astype(F32)
            for gq in range(2)
        ]
        mixed.append(jnp.concatenate(halves, axis=0))
    mixed = jnp.concatenate(mixed, axis=1) * inverse
    gates = u_ref[...].astype(F32)
    centered = mixed - jnp.mean(mixed, axis=1, keepdims=True)
    rstd = lax.rsqrt(jnp.mean(centered * centered, axis=1, keepdims=True) + EPS)
    normed = centered * rstd
    hid_ref[...] = (normed * gates).astype(BF16)
    grad_hidden = gh_ref[...]
    ghn_ref[...] = grad_hidden * normed
    grad_normed = grad_hidden * gates
    grad_mixed = rstd * (
        grad_normed
        - jnp.mean(grad_normed, axis=1, keepdims=True)
        - normed * jnp.mean(grad_normed * normed, axis=1, keepdims=True)
    )
    scaled = (grad_mixed * inverse).astype(BF16)
    for h in range(HEADS):
        for gq in range(2):
            for gk in range(2):
                send_ref[device(h, gq, gk), 0:SUB, :] = scaled[
                    gq * SUB : (gq + 1) * SUB, h * HEAD : (h + 1) * HEAD
                ]
    for j in range(D // HEAD):
        part = mm(hid_ref[...], cot_ref[:, j * HEAD : (j + 1) * HEAD], TN).astype(BF16)
        for d in range(NBLK):
            send_ref[d, SUB + j * 32 : SUB + (j + 1) * 32, :] = part[d * 32 : (d + 1) * 32]


def out_kernel(hid_ref, w_ref, out_ref):
    out_ref[...] = mm(hid_ref[...], w_ref[...], NN).astype(BF16)


def sum_kernel(parts_ref, gw_ref):
    total = parts_ref[0, SUB:, :].astype(F32)
    for d in range(1, NBLK):
        total = total + parts_ref[d, SUB:, :].astype(F32)
    gw_ref[...] = total.astype(BF16)


def backward_kernel(
    lens_ref, idx_ref, recv_ref, phiq_ref, phik_ref, grads_ref, freq_ref, send_ref,
    qp_s, gate_s, start_s, pos_s, sc_s, dqp_s, term_s,
):
    head, gq, gk = place(idx_ref)
    stage_rows(recv_ref, lens_ref, gq, qp_s, gate_s, start_s, pos_s)
    qp_s[:, HEAD:] = phiq_ref[...]
    for b in range(NBLK):
        sc_s[b * SUB : (b + 1) * SUB, :] = grads_ref[b, 0:SUB, :]
    freq = freq_ref[head].astype(BF16)
    freq = jnp.concatenate([freq, -freq], axis=1)
    dqp_s[...] = jnp.zeros_like(dqp_s)
    term_s[...] = jnp.zeros_like(term_s)

    def back(phi, grad_phi):
        turned = pltpu.roll(grad_phi, FREQS, 1)
        return mm((phi.astype(F32) * turned).astype(BF16), freq, NT)

    for c in range(TILES):
        rows = tile_rows(c)
        keys = tile_of(recv_ref, c, K0, V0)
        values = tile_of(recv_ref, c, V0, PACK)
        phik = phik_ref[c * TILE : (c + 1) * TILE, :]
        pairs = diagonal(keys, phik)
        scaled, gate = sc_s[rows, :], gate_s[rows, :]
        masked = masker(start_s, pos_s, rows, c, gk)
        both = mm(qp_s[rows, :], pairs, NT)
        half, kern = both[:, :TILE] * (0.5 * SCALE), both[:, TILE:]
        t = jnp.tanh(half)
        weights = half + half * t
        slope = (1.0 + t) + weights * (1.0 - t)
        grad_w = masked(mm(scaled, values, NT))
        both = masked(weights + gate * kern).astype(BF16)
        grad_s = (grad_w * slope * (0.5 * SCALE)).astype(BF16)
        grad_k = (grad_w * gate).astype(BF16)
        term_s[rows, :] += kern * grad_w
        dqp_s[rows, :] += mm(jnp.concatenate([grad_s, grad_k], axis=1), pairs, NN)
        dkey = mm(grad_s, qp_s[rows, :HEAD], TN)
        dkey = dkey + back(phik, mm(grad_k, qp_s[rows, HEAD:], TN))
        dval = mm(both, scaled, TN)
        for i in range(2):
            send_ref[2 * c + i, K0:V0, :] = dkey[i * SUB : (i + 1) * SUB].astype(BF16)
            send_ref[2 * c + i, V0:PACK, :] = dval[i * SUB : (i + 1) * SUB].astype(BF16)
    dq = dqp_s[:, :HEAD] + back(phiq_ref[...], dqp_s[:, HEAD:])
    gate = gate_s[...]
    term = jnp.sum(term_s[...], axis=1, keepdims=True) * gate * (1.0 - gate) * SCALE
    mine = lanes((SUB, HEAD)) == sublanes((SUB, HEAD))
    for b in range(NBLK):
        rows = slice(b * SUB, (b + 1) * SUB)
        send_ref[b, Q0:G0, :] = dq[rows].astype(BF16)
        across = jnp.sum(jnp.where(mine, term[rows], 0.0), axis=0, keepdims=True)
        send_ref[b, G0:K0, :] = jnp.broadcast_to(across, (16, HEAD)).astype(BF16)


def final_kernel(recv_ref, ghn_ref, gw_ref, dq_ref, dk_ref, dv_ref, dg_ref, dw_ref):
    mine = lanes((SUB, HEAD)) == sublanes((SUB, HEAD))

    def pair(one, two, first, last):
        return recv_ref[one, first:last, :].astype(F32) + recv_ref[two, first:last, :].astype(F32)

    for h in range(HEADS):
        cols = slice(h * HEAD, (h + 1) * HEAD)
        for i in range(2):
            rows = slice(i * SUB, (i + 1) * SUB)
            one, two = device(h, i, 0), device(h, i, 1)
            dq_ref[rows, cols] = pair(one, two, Q0, G0).astype(BF16)
            term = column(pair(one, two, G0, K0)[0:1], mine)
            dg_ref[rows, cols] = (ghn_ref[rows, cols] + term).astype(BF16)
            one, two = device(h, 0, i), device(h, 1, i)
            dk_ref[rows, cols] = pair(one, two, K0, V0).astype(BF16)
            dv_ref[rows, cols] = pair(one, two, V0, PACK).astype(BF16)
    for j in range(D // HEAD):
        dw_ref[:, j * HEAD : (j + 1) * HEAD] = gw_ref[j * 32 : (j + 1) * 32]


VMEM = pl.BlockSpec(memory_space=pltpu.VMEM)
SMEM = pl.BlockSpec(memory_space=pltpu.SMEM)
ANY = pl.BlockSpec(memory_space=pl.ANY)


def call(body, scalars, arrays, outs, scratch=(), us=1.0, space=VMEM, mib=16):
    return pl.pallas_call(
        body,
        in_specs=[SMEM] * len(scalars) + [space] * len(arrays),
        out_specs=[VMEM] * len(outs),
        out_shape=[jax.ShapeDtypeStruct(s, t) for s, t in outs],
        scratch_shapes=[pltpu.VMEM(*s) if isinstance(s, tuple) else s for s in scratch],
        compiler_params=pltpu.CompilerParams(vmem_limit_bytes=mib * 1024 * 1024),
        cost_estimate=pl.CostEstimate(
            flops=int(us * 1.1e9), bytes_accessed=1024, transcendentals=0
        ),
    )(*scalars, *arrays)


def swap(a, axis):
    return lax.all_to_all(a, axis, 0, 0, tiled=True)


def local(q, k, v, u, freqs, w, lens, cot):
    q, k, v, u, cot, lens = q[0], k[0], v[0], u[0], cot[0], lens[0]
    idx = lax.axis_index("blk").astype(jnp.int32)[None]
    staged = [
        ((ROWS, 2 * HEAD), BF16),
        ((ROWS, HEAD), F32),
        ((ROWS, HEAD), F32),
        ((ROWS, HEAD), F32),
    ]
    (send1,) = call(
        pack_kernel,
        [],
        [q, k, v, u],
        [((NBLK, PACK, HEAD), BF16)],
        [((TOK, WIDTH), BF16)] * 4 + [pltpu.SemaphoreType.DMA((4,))],
        space=ANY,
        mib=60,
    )
    recv1 = swap(send1, "blk")
    (gh,) = call(hidden_grad_kernel, [], [w, cot], [((TOK, WIDTH), F32)])
    mixed, phiq, phik = call(
        forward_kernel,
        [lens, idx],
        [recv1, freqs],
        [((NBLK, SUB, HEAD), BF16), ((ROWS, HEAD), BF16), ((ROWS, HEAD), BF16)],
        staged + [((ROWS, HEAD), F32)],
        us=4.5,
    )
    recv2 = swap(mixed, "blk")
    hidden, send3, ghn = call(
        middle_kernel,
        [lens, idx],
        [recv2, u, gh, cot],
        [((TOK, WIDTH), BF16), ((NBLK, SUB + WROWS, HEAD), BF16), ((TOK, WIDTH), F32)],
    )
    recv3 = swap(send3, "blk")
    (gw,) = call(sum_kernel, [], [recv3], [((WROWS, HEAD), BF16)])
    (layer_out,) = call(out_kernel, [], [hidden, w], [((TOK, D), BF16)])
    (send4,) = call(
        backward_kernel,
        [lens, idx],
        [recv1, phiq, phik, recv3, freqs],
        [((NBLK, PACK, HEAD), BF16)],
        staged + [((ROWS, HEAD), BF16), ((ROWS, 2 * HEAD), F32), ((ROWS, HEAD), F32)],
        us=5.5,
    )
    for mask in (8, 1, 2, 4):
        other = lax.ppermute(gw, "dp", [(i, i ^ mask) for i in range(16)])
        gw = gw.astype(F32) + other.astype(F32)
        if mask != 4:
            gw = gw.astype(BF16)
        if mask == 8:
            send4, gw = lax.optimization_barrier((send4, gw))
    recv4 = swap(send4, "blk")
    dq, dk, dv, dg, dw = call(
        final_kernel,
        [],
        [recv4, ghn, gw],
        [((TOK, WIDTH), BF16)] * 4 + [((WIDTH // NBLK, D), F32)],
    )
    return layer_out[None], dq[None], dk[None], dv[None], dg[None], dw


def solution(mesh):
    rows = P("dp", "blk", None)
    return jax.shard_map(
        local,
        mesh=mesh,
        in_specs=(rows, rows, rows, rows, P(), P(), P("dp", None), rows),
        out_specs=(rows, rows, rows, rows, rows, P("blk", None)),
        check_vma=False,
    )
```

```python
import math

import jax
import jax.numpy as jnp
from jax import lax
from jax.experimental import pallas as pl
from jax.experimental.pallas import tpu as pltpu
from jax.sharding import PartitionSpec as P

EPS = 1e-05
HEADS, HEAD, FREQS, USERS = 4, 128, 64, 8
TOK, NBLK = 128, 16
SUB = TOK // 2
WIDTH, D = HEADS * HEAD, 1024
ROWS = SUB * NBLK
TILE = 2 * SUB
REACH = 5
TILES = ROWS // TILE
SCALE = 1.0 / math.sqrt(HEAD)
F32, BF16 = jnp.float32, jnp.bfloat16

Q0, G0, K0, V0, PACK = 0, SUB, SUB + 16, 2 * SUB + 16, 3 * SUB + 16
WROWS = (WIDTH // NBLK) * D // HEAD


def device(h, gq, gk):
    return 4 * h + 2 * gq + gk


NT = (((1,), (1,)), ((), ()))
NN = (((1,), (0,)), ((), ()))
TN = (((0,), (0,)), ((), ()))


def mm(a, b, dims):
    return lax.dot_general(a, b, dims, preferred_element_type=F32)


def lanes(shape):
    return lax.broadcasted_iota(jnp.int32, shape, 1)


def sublanes(shape):
    return lax.broadcasted_iota(jnp.int32, shape, 0)


def column(row, mine):
    return jnp.sum(jnp.where(mine, row, 0.0), axis=1, keepdims=True)


def starts_of(lens_ref, pos):
    end = jnp.int32(0)
    start = jnp.zeros_like(pos)
    for u in range(USERS):
        end = end + lens_ref[u]
        start = jnp.where(pos >= end, end, start)
    return start


def cos_sin(angles):
    turns = jnp.floor(angles * (2.0 / math.pi) + 0.5)
    r = angles - turns * 1.5703125
    r = r - turns * 4.837512969970703125e-4
    r = r - turns * 7.54978995489188e-8
    quad = turns.astype(jnp.int32) - jnp.where(lanes(angles.shape) >= FREQS, 1, 0)
    z = r * r
    c = 1.0 - 0.5 * z + z * z * (4.166664568e-2 + z * (-1.388731625e-3 + z * 2.443315712e-5))
    s = r + r * z * (-1.6666654611e-1 + z * (8.3321608736e-3 - z * 1.9515295891e-4))
    odd = (quad & 1) == 1
    value = jnp.where(odd, s, c)
    return jnp.where(((quad + 1) & 2) == 2, -value, value)


def pack_kernel(q_hbm, k_hbm, v_hbm, u_hbm, out_ref, q_ref, k_ref, v_ref, u_ref, sems):
    pairs = ((u_hbm, u_ref), (q_hbm, q_ref), (k_hbm, k_ref), (v_hbm, v_ref))
    copies = [pltpu.make_async_copy(src, dst, sems.at[i]) for i, (src, dst) in enumerate(pairs)]
    for copy in copies:
        copy.start()
    ones = jnp.ones((16, HEAD), BF16)
    copies[0].wait()
    for h in range(HEADS):
        total = mm(ones, u_ref[:, h * HEAD : (h + 1) * HEAD], NT)
        gate = jax.nn.sigmoid(total * SCALE)
        high = gate.astype(BF16).astype(F32)
        gate = jnp.where(sublanes((16, TOK)) < 8, high, gate - high).astype(BF16)
        for d in range(device(h, 0, 0), device(h, 1, 1) + 1):
            out_ref[d, G0:K0, :] = gate
    for copy in copies[1:]:
        copy.wait()
    for h in range(HEADS):
        cols = slice(h * HEAD, (h + 1) * HEAD)
        for gq in range(2):
            for gk in range(2):
                d = device(h, gq, gk)
                out_ref[d, Q0:G0, :] = q_ref[gq * SUB : (gq + 1) * SUB, cols]
                out_ref[d, K0:V0, :] = k_ref[gk * SUB : (gk + 1) * SUB, cols]
                out_ref[d, V0:PACK, :] = v_ref[gk * SUB : (gk + 1) * SUB, cols]


def stage_rows(recv_ref, lens_ref, gq, qp_s, gate_s, start_s, pos_s):
    pos = sublanes((NBLK, TOK)) * TOK + lanes((NBLK, TOK))
    starts = starts_of(lens_ref, pos).astype(F32)
    first = (sublanes((SUB, HEAD)) + gq * SUB).astype(F32)
    mine = lanes((SUB, TOK)) == sublanes((SUB, TOK)) + gq * SUB
    for b in range(NBLK):
        rows = slice(b * SUB, (b + 1) * SUB)
        qp_s[rows, :HEAD] = recv_ref[b, Q0:G0, :]
        parts = recv_ref[b, G0:K0, :].astype(F32)
        gate_s[rows, :] = jnp.broadcast_to(column(parts[0:1] + parts[8:9], mine), (SUB, HEAD))
        start_s[rows, :] = jnp.broadcast_to(column(starts[b : b + 1], mine), (SUB, HEAD))
        pos_s[rows, :] = first + float(b * TOK)


def tile_of(recv_ref, c, first, last):
    return jnp.concatenate(
        [recv_ref[2 * c, first:last, :], recv_ref[2 * c + 1, first:last, :]], axis=0
    )


def diagonal(a, b):
    zero = jnp.zeros_like(a)
    return jnp.concatenate(
        [jnp.concatenate([a, zero], axis=1), jnp.concatenate([zero, b], axis=1)], axis=0
    )


def masker(start_s, pos_s, rows, c, gk):
    lane = lanes((1, TILE))
    key = ((2 * c + (lane >> 6)) * TOK + gk * SUB + (lane & (SUB - 1))).astype(F32)
    top = slice(rows.start, rows.start + TILE)
    near = (key >= start_s[top, :]) & (key <= pos_s[top, :])
    if rows.stop == top.stop:
        return lambda x: jnp.where(near, x, 0.0)
    far = key >= start_s[top.stop : rows.stop, :]

    def masked(x):
        return jnp.concatenate(
            [jnp.where(near, x[:TILE], 0.0), jnp.where(far, x[TILE:], 0.0)], axis=0
        )

    return masked


def place(idx_ref):
    return idx_ref[0] // 4, (idx_ref[0] // 2) % 2, idx_ref[0] % 2


def tile_rows(c):
    return slice(c * TILE, min(c + REACH, TILES) * TILE)


def forward_kernel(
    lens_ref, idx_ref, recv_ref, freq_ref, mixed_ref, phiq_ref, phik_ref,
    qp_s, gate_s, start_s, pos_s, acc_s,
):
    head, gq, gk = place(idx_ref)
    stage_rows(recv_ref, lens_ref, gq, qp_s, gate_s, start_s, pos_s)
    freq = freq_ref[head]
    freq = jnp.concatenate([freq, freq], axis=1)
    pieces = []
    for _ in range(3):
        piece = freq.astype(BF16)
        pieces.append(piece)
        freq = freq - piece.astype(F32)
    pieces = jnp.concatenate(pieces, axis=1)

    def phi_of(x):
        a = mm(x, pieces, NN)
        angles = (a[:, 2 * HEAD :] + a[:, HEAD : 2 * HEAD]) + a[:, :HEAD]
        return (cos_sin(angles) / math.sqrt(FREQS)).astype(BF16)

    for i in range(4):
        rows = slice(i * ROWS // 4, (i + 1) * ROWS // 4)
        phiq = phi_of(qp_s[rows, :HEAD])
        phiq_ref[rows, :] = phiq
        qp_s[rows, HEAD:] = phiq
    acc_s[...] = jnp.zeros_like(acc_s)
    for c in range(TILES):
        rows = tile_rows(c)
        keys = tile_of(recv_ref, c, K0, V0)
        values = tile_of(recv_ref, c, V0, PACK)
        phik = phi_of(keys)
        phik_ref[c * TILE : (c + 1) * TILE, :] = phik
        both = mm(qp_s[rows, :], diagonal(keys, phik), NT)
        half, kern = both[:, :TILE] * (0.5 * SCALE), both[:, TILE:]
        both = half + half * jnp.tanh(half) + gate_s[rows, :] * kern
        both = masker(start_s, pos_s, rows, c, gk)(both).astype(BF16)
        acc_s[rows, :] += mm(both, values, NN)
    for b in range(NBLK):
        mixed_ref[b] = acc_s[b * SUB : (b + 1) * SUB, :].astype(BF16)


def hidden_grad_kernel(w_ref, cot_ref, gh_ref):
    gh_ref[...] = mm(cot_ref[...], w_ref[...], NT)


def middle_kernel(
    lens_ref, idx_ref, mixed_ref, u_ref, gh_ref, cot_ref, hid_ref, send_ref, ghn_ref
):
    pos = idx_ref[0] * TOK + sublanes((TOK, HEAD))
    count = (pos - starts_of(lens_ref, pos) + 1).astype(F32)
    inverse = jnp.concatenate([1.0 / count] * HEADS, axis=1)
    mixed = []
    for h in range(HEADS):
        halves = [
            mixed_ref[device(h, gq, 0)].astype(F32) + mixed_ref[device(h, gq, 1)].astype(F32)
            for gq in range(2)
        ]
        mixed.append(jnp.concatenate(halves, axis=0))
    mixed = jnp.concatenate(mixed, axis=1) * inverse
    gates = u_ref[...].astype(F32)
    centered = mixed - jnp.mean(mixed, axis=1, keepdims=True)
    rstd = lax.rsqrt(jnp.mean(centered * centered, axis=1, keepdims=True) + EPS)
    normed = centered * rstd
    hid_ref[...] = (normed * gates).astype(BF16)
    grad_hidden = gh_ref[...]
    ghn_ref[...] = grad_hidden * normed
    grad_normed = grad_hidden * gates
    grad_mixed = rstd * (
        grad_normed
        - jnp.mean(grad_normed, axis=1, keepdims=True)
        - normed * jnp.mean(grad_normed * normed, axis=1, keepdims=True)
    )
    scaled = (grad_mixed * inverse).astype(BF16)
    for h in range(HEADS):
        for gq in range(2):
            for gk in range(2):
                send_ref[device(h, gq, gk), 0:SUB, :] = scaled[
                    gq * SUB : (gq + 1) * SUB, h * HEAD : (h + 1) * HEAD
                ]
    for j in range(D // HEAD):
        part = mm(hid_ref[...], cot_ref[:, j * HEAD : (j + 1) * HEAD], TN).astype(BF16)
        for d in range(NBLK):
            send_ref[d, SUB + j * 32 : SUB + (j + 1) * 32, :] = part[d * 32 : (d + 1) * 32]


def out_kernel(hid_ref, w_ref, out_ref):
    out_ref[...] = mm(hid_ref[...], w_ref[...], NN).astype(BF16)


def sum_kernel(parts_ref, gw_ref):
    total = parts_ref[0, SUB:, :].astype(F32)
    for d in range(1, NBLK):
        total = total + parts_ref[d, SUB:, :].astype(F32)
    gw_ref[...] = total.astype(BF16)


def add_kernel(one_ref, two_ref, out_ref):
    total = one_ref[...].astype(F32) + two_ref[...].astype(F32)
    out_ref[...] = total.astype(out_ref.dtype)


def backward_kernel(
    lens_ref, idx_ref, recv_ref, phiq_ref, phik_ref, grads_ref, freq_ref, send_ref,
    qp_s, gate_s, start_s, pos_s, sc_s, dqp_s, term_s,
):
    head, gq, gk = place(idx_ref)
    stage_rows(recv_ref, lens_ref, gq, qp_s, gate_s, start_s, pos_s)
    qp_s[:, HEAD:] = phiq_ref[...]
    for b in range(NBLK):
        sc_s[b * SUB : (b + 1) * SUB, :] = grads_ref[b, 0:SUB, :]
    freq = freq_ref[head].astype(BF16)
    freq = jnp.concatenate([freq, -freq], axis=1)
    dqp_s[...] = jnp.zeros_like(dqp_s)
    term_s[...] = jnp.zeros_like(term_s)

    def back(phi, grad_phi):
        turned = pltpu.roll(grad_phi, FREQS, 1)
        return mm((phi.astype(F32) * turned).astype(BF16), freq, NT)

    for c in range(TILES):
        rows = tile_rows(c)
        keys = tile_of(recv_ref, c, K0, V0)
        values = tile_of(recv_ref, c, V0, PACK)
        phik = phik_ref[c * TILE : (c + 1) * TILE, :]
        pairs = diagonal(keys, phik)
        scaled, gate = sc_s[rows, :], gate_s[rows, :]
        masked = masker(start_s, pos_s, rows, c, gk)
        both = mm(qp_s[rows, :], pairs, NT)
        half, kern = both[:, :TILE] * (0.5 * SCALE), both[:, TILE:]
        t = jnp.tanh(half)
        weights = half + half * t
        slope = (1.0 + t) + weights * (1.0 - t)
        grad_w = masked(mm(scaled, values, NT))
        both = masked(weights + gate * kern).astype(BF16)
        grad_s = (grad_w * slope * (0.5 * SCALE)).astype(BF16)
        grad_k = (grad_w * gate).astype(BF16)
        term_s[rows, :] += kern * grad_w
        dqp_s[rows, :] += mm(jnp.concatenate([grad_s, grad_k], axis=1), pairs, NN)
        dkey = mm(grad_s, qp_s[rows, :HEAD], TN)
        dkey = dkey + back(phik, mm(grad_k, qp_s[rows, HEAD:], TN))
        dval = mm(both, scaled, TN)
        for i in range(2):
            send_ref[2 * c + i, K0:V0, :] = dkey[i * SUB : (i + 1) * SUB].astype(BF16)
            send_ref[2 * c + i, V0:PACK, :] = dval[i * SUB : (i + 1) * SUB].astype(BF16)
    dq = dqp_s[:, :HEAD] + back(phiq_ref[...], dqp_s[:, HEAD:])
    gate = gate_s[...]
    term = jnp.sum(term_s[...], axis=1, keepdims=True) * gate * (1.0 - gate) * SCALE
    mine = lanes((SUB, HEAD)) == sublanes((SUB, HEAD))
    for b in range(NBLK):
        rows = slice(b * SUB, (b + 1) * SUB)
        send_ref[b, Q0:G0, :] = dq[rows].astype(BF16)
        across = jnp.sum(jnp.where(mine, term[rows], 0.0), axis=0, keepdims=True)
        send_ref[b, G0:K0, :] = jnp.broadcast_to(across, (16, HEAD)).astype(BF16)


def final_kernel(recv_ref, ghn_ref, gw_ref, dq_ref, dk_ref, dv_ref, dg_ref, dw_ref):
    mine = lanes((SUB, HEAD)) == sublanes((SUB, HEAD))

    def pair(one, two, first, last):
        return recv_ref[one, first:last, :].astype(F32) + recv_ref[two, first:last, :].astype(F32)

    for h in range(HEADS):
        cols = slice(h * HEAD, (h + 1) * HEAD)
        for i in range(2):
            rows = slice(i * SUB, (i + 1) * SUB)
            one, two = device(h, i, 0), device(h, i, 1)
            dq_ref[rows, cols] = pair(one, two, Q0, G0).astype(BF16)
            term = column(pair(one, two, G0, K0)[0:1], mine)
            dg_ref[rows, cols] = (ghn_ref[rows, cols] + term).astype(BF16)
            one, two = device(h, 0, i), device(h, 1, i)
            dk_ref[rows, cols] = pair(one, two, K0, V0).astype(BF16)
            dv_ref[rows, cols] = pair(one, two, V0, PACK).astype(BF16)
    for j in range(D // HEAD):
        dw_ref[:, j * HEAD : (j + 1) * HEAD] = gw_ref[j * 32 : (j + 1) * 32]


VMEM = pl.BlockSpec(memory_space=pltpu.VMEM)
SMEM = pl.BlockSpec(memory_space=pltpu.SMEM)
ANY = pl.BlockSpec(memory_space=pl.ANY)


def call(body, scalars, arrays, outs, scratch=(), us=1.0, space=VMEM, mib=16, after=()):
    if after:
        inner, first = body, len(scalars) + len(arrays)

        def body(*refs):
            inner(*refs[:first], *refs[first + len(after) :])

    moved = sum(x.size * x.dtype.itemsize for x in arrays)
    moved += sum(math.prod(s) * jnp.dtype(t).itemsize for s, t in outs)
    return pl.pallas_call(
        body,
        in_specs=[SMEM] * len(scalars) + [space] * len(arrays) + [ANY] * len(after),
        out_specs=[VMEM] * len(outs),
        out_shape=[jax.ShapeDtypeStruct(s, t) for s, t in outs],
        scratch_shapes=[pltpu.VMEM(*s) if isinstance(s, tuple) else s for s in scratch],
        compiler_params=pltpu.CompilerParams(vmem_limit_bytes=mib * 1024 * 1024),
        cost_estimate=pl.CostEstimate(
            flops=int(us * 1.1e9), bytes_accessed=moved, transcendentals=0
        ),
    )(*scalars, *arrays, *after)


def swap(a, axis):
    return lax.all_to_all(a, axis, 0, 0, tiled=True)


def local(q, k, v, u, freqs, w, lens, cot):
    q, k, v, u, cot, lens = q[0], k[0], v[0], u[0], cot[0], lens[0]
    idx = lax.axis_index("blk").astype(jnp.int32)[None]
    staged = [
        ((ROWS, 2 * HEAD), BF16),
        ((ROWS, HEAD), F32),
        ((ROWS, HEAD), F32),
        ((ROWS, HEAD), F32),
    ]
    (send1,) = call(
        pack_kernel,
        [],
        [q, k, v, u],
        [((NBLK, PACK, HEAD), BF16)],
        [((TOK, WIDTH), BF16)] * 4 + [pltpu.SemaphoreType.DMA((4,))],
        space=ANY,
        mib=60,
    )
    recv1 = swap(send1, "blk")
    (gh,) = call(hidden_grad_kernel, [], [w, cot], [((TOK, WIDTH), F32)])
    mixed, phiq, phik = call(
        forward_kernel,
        [lens, idx],
        [recv1, freqs],
        [((NBLK, SUB, HEAD), BF16), ((ROWS, HEAD), BF16), ((ROWS, HEAD), BF16)],
        staged + [((ROWS, HEAD), F32)],
        after=[gh],
        us=4.5,
    )
    recv2 = swap(mixed, "blk")
    hidden, send3, ghn = call(
        middle_kernel,
        [lens, idx],
        [recv2, u, gh, cot],
        [((TOK, WIDTH), BF16), ((NBLK, SUB + WROWS, HEAD), BF16), ((TOK, WIDTH), F32)],
    )
    recv3 = swap(send3, "blk")
    (gw,) = call(sum_kernel, [], [recv3], [((WROWS, HEAD), BF16)])
    (layer_out,) = call(out_kernel, [], [hidden, w], [((TOK, D), BF16)])
    (send4,) = call(
        backward_kernel,
        [lens, idx],
        [recv1, phiq, phik, recv3, freqs],
        [((NBLK, PACK, HEAD), BF16)],
        staged + [((ROWS, HEAD), BF16), ((ROWS, 2 * HEAD), F32), ((ROWS, HEAD), F32)],
        us=5.5,
    )
    for mask in (8, 1, 2, 4):
        other = lax.ppermute(gw, "dp", [(i, i ^ mask) for i in range(16)])
        kind = F32 if mask == 4 else BF16
        (gw,) = call(add_kernel, [], [gw, other], [((WROWS, HEAD), kind)], us=0.5)
        if mask == 8:
            send4, gw = lax.optimization_barrier((send4, gw))
    recv4 = swap(send4, "blk")
    dq, dk, dv, dg, dw = call(
        final_kernel,
        [],
        [recv4, ghn, gw],
        [((TOK, WIDTH), BF16)] * 4 + [((WIDTH // NBLK, D), F32)],
    )
    return layer_out[None], dq[None], dk[None], dv[None], dg[None], dw


def solution(mesh):
    rows = P("dp", "blk", None)
    return jax.shard_map(
        local,
        mesh=mesh,
        in_specs=(rows, rows, rows, rows, P(), P(), P("dp", None), rows),
        out_specs=(rows, rows, rows, rows, rows, P("blk", None)),
        check_vma=False,
    )
```

```python
import math

import jax
import jax.numpy as jnp
from jax import lax
from jax.experimental import pallas as pl
from jax.experimental.pallas import tpu as pltpu
from jax.sharding import PartitionSpec as P

EPS = 1e-05
HEADS, HEAD, FREQS, USERS = 4, 128, 64, 8
TOK, NBLK = 128, 16
SUB = TOK // 2
WIDTH, D = HEADS * HEAD, 1024
ROWS = SUB * NBLK
TILE = 2 * SUB
REACH = 5
TILES = ROWS // TILE
SCALE = 1.0 / math.sqrt(HEAD)
F32, BF16 = jnp.float32, jnp.bfloat16

Q0, G0, K0, V0, PACK = 0, SUB, SUB + 16, 2 * SUB + 16, 3 * SUB + 16
WROWS = (WIDTH // NBLK) * D // HEAD


def device(h, gq, gk):
    return 4 * h + 2 * gq + gk


NT = (((1,), (1,)), ((), ()))
NN = (((1,), (0,)), ((), ()))
TN = (((0,), (0,)), ((), ()))


def mm(a, b, dims):
    return lax.dot_general(a, b, dims, preferred_element_type=F32)


def lanes(shape):
    return lax.broadcasted_iota(jnp.int32, shape, 1)


def sublanes(shape):
    return lax.broadcasted_iota(jnp.int32, shape, 0)


def column(row, mine):
    return jnp.sum(jnp.where(mine, row, 0.0), axis=1, keepdims=True)


def starts_of(lens_ref, pos):
    end = jnp.int32(0)
    start = jnp.zeros_like(pos)
    for u in range(USERS):
        end = end + lens_ref[u]
        start = jnp.where(pos >= end, end, start)
    return start


def cos_sin(angles):
    turns = jnp.floor(angles * (2.0 / math.pi) + 0.5)
    r = angles - turns * 1.5703125
    r = r - turns * 4.837512969970703125e-4
    r = r - turns * 7.54978995489188e-8
    quad = turns.astype(jnp.int32) - jnp.where(lanes(angles.shape) >= FREQS, 1, 0)
    z = r * r
    c = 1.0 - 0.5 * z + z * z * (4.166664568e-2 + z * (-1.388731625e-3 + z * 2.443315712e-5))
    s = r + r * z * (-1.6666654611e-1 + z * (8.3321608736e-3 - z * 1.9515295891e-4))
    odd = (quad & 1) == 1
    value = jnp.where(odd, s, c)
    return jnp.where(((quad + 1) & 2) == 2, -value, value)


def pack_kernel(q_hbm, k_hbm, v_hbm, u_hbm, out_ref, q_ref, k_ref, v_ref, u_ref, sems):
    pairs = ((u_hbm, u_ref), (q_hbm, q_ref), (k_hbm, k_ref), (v_hbm, v_ref))
    copies = [pltpu.make_async_copy(src, dst, sems.at[i]) for i, (src, dst) in enumerate(pairs)]
    for copy in copies:
        copy.start()
    ones = jnp.ones((16, HEAD), BF16)
    copies[0].wait()
    for h in range(HEADS):
        total = mm(ones, u_ref[:, h * HEAD : (h + 1) * HEAD], NT)
        gate = jax.nn.sigmoid(total * SCALE)
        high = gate.astype(BF16).astype(F32)
        gate = jnp.where(sublanes((16, TOK)) < 8, high, gate - high).astype(BF16)
        for d in range(device(h, 0, 0), device(h, 1, 1) + 1):
            out_ref[d, G0:K0, :] = gate
    for copy in copies[1:]:
        copy.wait()
    for h in range(HEADS):
        cols = slice(h * HEAD, (h + 1) * HEAD)
        for gq in range(2):
            for gk in range(2):
                d = device(h, gq, gk)
                out_ref[d, Q0:G0, :] = q_ref[gq * SUB : (gq + 1) * SUB, cols]
                out_ref[d, K0:V0, :] = k_ref[gk * SUB : (gk + 1) * SUB, cols]
                out_ref[d, V0:PACK, :] = v_ref[gk * SUB : (gk + 1) * SUB, cols]


def stage_rows(recv_ref, lens_ref, gq, qp_s, gate_s, start_s, pos_s):
    pos = sublanes((NBLK, TOK)) * TOK + lanes((NBLK, TOK))
    starts = starts_of(lens_ref, pos).astype(F32)
    first = (sublanes((SUB, HEAD)) + gq * SUB).astype(F32)
    mine = lanes((SUB, TOK)) == sublanes((SUB, TOK)) + gq * SUB
    for b in range(NBLK):
        rows = slice(b * SUB, (b + 1) * SUB)
        qp_s[rows, :HEAD] = recv_ref[b, Q0:G0, :]
        parts = recv_ref[b, G0:K0, :].astype(F32)
        gate_s[rows, :] = jnp.broadcast_to(column(parts[0:1] + parts[8:9], mine), (SUB, HEAD))
        start_s[rows, :] = jnp.broadcast_to(column(starts[b : b + 1], mine), (SUB, HEAD))
        pos_s[rows, :] = first + float(b * TOK)


def tile_of(recv_ref, c, first, last):
    return jnp.concatenate(
        [recv_ref[2 * c, first:last, :], recv_ref[2 * c + 1, first:last, :]], axis=0
    )


def diagonal(a, b):
    zero = jnp.zeros_like(a)
    return jnp.concatenate(
        [jnp.concatenate([a, zero], axis=1), jnp.concatenate([zero, b], axis=1)], axis=0
    )


def masker(start_s, pos_s, rows, c, gk):
    lane = lanes((1, TILE))
    key = ((2 * c + (lane >> 6)) * TOK + gk * SUB + (lane & (SUB - 1))).astype(F32)
    top = slice(rows.start, rows.start + TILE)
    near = (key >= start_s[top, :]) & (key <= pos_s[top, :])
    if rows.stop == top.stop:
        return lambda x: jnp.where(near, x, 0.0)
    far = key >= start_s[top.stop : rows.stop, :]

    def masked(x):
        return jnp.concatenate(
            [jnp.where(near, x[:TILE], 0.0), jnp.where(far, x[TILE:], 0.0)], axis=0
        )

    return masked


def place(idx_ref):
    return idx_ref[0] // 4, (idx_ref[0] // 2) % 2, idx_ref[0] % 2


def tile_rows(c):
    return slice(c * TILE, min(c + REACH, TILES) * TILE)


def forward_kernel(
    lens_ref, idx_ref, recv_ref, freq_ref, mixed_ref, phiq_ref, phik_ref,
    qp_s, gate_s, start_s, pos_s, acc_s,
):
    head, gq, gk = place(idx_ref)
    stage_rows(recv_ref, lens_ref, gq, qp_s, gate_s, start_s, pos_s)
    freq = freq_ref[head]
    freq = jnp.concatenate([freq, freq], axis=1)
    pieces = []
    for _ in range(3):
        piece = freq.astype(BF16)
        pieces.append(piece)
        freq = freq - piece.astype(F32)
    pieces = jnp.concatenate(pieces, axis=1)

    def phi_of(x):
        a = mm(x, pieces, NN)
        angles = (a[:, 2 * HEAD :] + a[:, HEAD : 2 * HEAD]) + a[:, :HEAD]
        return (cos_sin(angles) / math.sqrt(FREQS)).astype(BF16)

    for i in range(4):
        rows = slice(i * ROWS // 4, (i + 1) * ROWS // 4)
        phiq = phi_of(qp_s[rows, :HEAD])
        phiq_ref[rows, :] = phiq
        qp_s[rows, HEAD:] = phiq
    acc_s[...] = jnp.zeros_like(acc_s)
    for c in range(TILES):
        rows = tile_rows(c)
        keys = tile_of(recv_ref, c, K0, V0)
        values = tile_of(recv_ref, c, V0, PACK)
        phik = phi_of(keys)
        phik_ref[c * TILE : (c + 1) * TILE, :] = phik
        both = mm(qp_s[rows, :], diagonal(keys, phik), NT)
        half, kern = both[:, :TILE] * (0.5 * SCALE), both[:, TILE:]
        both = half + half * jnp.tanh(half) + gate_s[rows, :] * kern
        both = masker(start_s, pos_s, rows, c, gk)(both).astype(BF16)
        acc_s[rows, :] += mm(both, values, NN)
    for b in range(NBLK):
        mixed_ref[b] = acc_s[b * SUB : (b + 1) * SUB, :].astype(BF16)


def hidden_grad_kernel(w_ref, cot_ref, gh_ref):
    gh_ref[...] = mm(cot_ref[...], w_ref[...], NT)


def norm_kernel(lens_ref, idx_ref, mixed_ref, u_ref, hid_ref, normed_ref, scales_ref):
    pos = idx_ref[0] * TOK + sublanes((TOK, HEAD))
    count = (pos - starts_of(lens_ref, pos) + 1).astype(F32)
    inverse = jnp.concatenate([1.0 / count] * HEADS, axis=1)
    mixed = []
    for h in range(HEADS):
        halves = [
            mixed_ref[device(h, gq, 0)].astype(F32) + mixed_ref[device(h, gq, 1)].astype(F32)
            for gq in range(2)
        ]
        mixed.append(jnp.concatenate(halves, axis=0))
    mixed = jnp.concatenate(mixed, axis=1) * inverse
    gates = u_ref[...].astype(F32)
    centered = mixed - jnp.mean(mixed, axis=1, keepdims=True)
    rstd = lax.rsqrt(jnp.mean(centered * centered, axis=1, keepdims=True) + EPS)
    normed = centered * rstd
    hid_ref[...] = (normed * gates).astype(BF16)
    normed_ref[...] = normed
    scales_ref[:, :HEAD] = jnp.broadcast_to(rstd, (TOK, HEAD))
    scales_ref[:, HEAD:] = inverse[:, :HEAD]


def scale_kernel(u_ref, gh_ref, normed_ref, scales_ref, scaled_ref, ghn_ref):
    gates, normed, grad_hidden = u_ref[...].astype(F32), normed_ref[...], gh_ref[...]
    rstd = jnp.concatenate([scales_ref[:, :HEAD]] * HEADS, axis=1)
    inverse = jnp.concatenate([scales_ref[:, HEAD:]] * HEADS, axis=1)
    ghn_ref[...] = grad_hidden * normed
    grad_normed = grad_hidden * gates
    grad_mixed = rstd * (
        grad_normed
        - jnp.mean(grad_normed, axis=1, keepdims=True)
        - normed * jnp.mean(grad_normed * normed, axis=1, keepdims=True)
    )
    scaled_ref[...] = (grad_mixed * inverse).astype(BF16)


def weight_kernel(idx_ref, scaled_ref, hid_ref, hid2_ref, cot_ref, cot2_ref, send_ref):
    for h in range(HEADS):
        for gq in range(2):
            for gk in range(2):
                send_ref[device(h, gq, gk), 0:SUB, :] = scaled_ref[
                    gq * SUB : (gq + 1) * SUB, h * HEAD : (h + 1) * HEAD
                ]
    hidden = jnp.concatenate([hid_ref[...], hid2_ref[...]], axis=0)
    first = (idx_ref[0] % 2) * (D // 2)
    for j in range(D // 2 // 256):
        cols = pl.ds(pl.multiple_of(first + j * 256, 256), 256)
        cots = jnp.concatenate([cot_ref[:, cols], cot2_ref[:, cols]], axis=0)
        part = mm(hidden, cots, TN).astype(BF16)
        for i in range(2):
            top = SUB + (2 * j + i) * 32
            for d in range(NBLK):
                send_ref[d, top : top + 32, :] = part[
                    d * 32 : (d + 1) * 32, i * HEAD : (i + 1) * HEAD
                ]


def out_kernel(hid_ref, w_ref, out_ref):
    out_ref[...] = mm(hid_ref[...], w_ref[...], NN).astype(BF16)


def sum_kernel(parts_ref, gw_ref):
    for half in range(2):
        total = parts_ref[half, SUB:, :].astype(F32)
        for d in range(half + 2, NBLK, 2):
            total = total + parts_ref[d, SUB:, :].astype(F32)
        gw_ref[half * WROWS // 2 : (half + 1) * WROWS // 2, :] = total.astype(BF16)


def add_kernel(*refs):
    parts = [ref[...].astype(F32) for ref in refs[:-1]]
    total = parts[0] + parts[1]
    if len(parts) == 4:
        total = total + (parts[2] + parts[3])
    refs[-1][...] = total.astype(refs[-1].dtype)


def backward_kernel(
    lens_ref, idx_ref, recv_ref, phiq_ref, phik_ref, grads_ref, freq_ref, send_ref,
    qp_s, gate_s, start_s, pos_s, sc_s, dqp_s, term_s,
):
    head, gq, gk = place(idx_ref)
    stage_rows(recv_ref, lens_ref, gq, qp_s, gate_s, start_s, pos_s)
    qp_s[:, HEAD:] = phiq_ref[...]
    for b in range(NBLK):
        sc_s[b * SUB : (b + 1) * SUB, :] = grads_ref[b, 0:SUB, :]
    freq = freq_ref[head].astype(BF16)
    freq = jnp.concatenate([freq, -freq], axis=1)
    dqp_s[...] = jnp.zeros_like(dqp_s)
    term_s[...] = jnp.zeros_like(term_s)

    def back(phi, grad_phi):
        turned = pltpu.roll(grad_phi, FREQS, 1)
        return mm((phi.astype(F32) * turned).astype(BF16), freq, NT)

    for c in range(TILES):
        rows = tile_rows(c)
        keys = tile_of(recv_ref, c, K0, V0)
        values = tile_of(recv_ref, c, V0, PACK)
        phik = phik_ref[c * TILE : (c + 1) * TILE, :]
        pairs = diagonal(keys, phik)
        scaled, gate = sc_s[rows, :], gate_s[rows, :]
        masked = masker(start_s, pos_s, rows, c, gk)
        both = mm(qp_s[rows, :], pairs, NT)
        half, kern = both[:, :TILE] * (0.5 * SCALE), both[:, TILE:]
        t = jnp.tanh(half)
        weights = half + half * t
        slope = (1.0 + t) + weights * (1.0 - t)
        grad_w = masked(mm(scaled, values, NT))
        both = masked(weights + gate * kern).astype(BF16)
        grad_s = (grad_w * slope * (0.5 * SCALE)).astype(BF16)
        grad_k = (grad_w * gate).astype(BF16)
        term_s[rows, :] += kern * grad_w
        dqp_s[rows, :] += mm(jnp.concatenate([grad_s, grad_k], axis=1), pairs, NN)
        dkey = mm(grad_s, qp_s[rows, :HEAD], TN)
        dkey = dkey + back(phik, mm(grad_k, qp_s[rows, HEAD:], TN))
        dval = mm(both, scaled, TN)
        for i in range(2):
            send_ref[2 * c + i, K0:V0, :] = dkey[i * SUB : (i + 1) * SUB].astype(BF16)
            send_ref[2 * c + i, V0:PACK, :] = dval[i * SUB : (i + 1) * SUB].astype(BF16)
    dq = dqp_s[:, :HEAD] + back(phiq_ref[...], dqp_s[:, HEAD:])
    gate = gate_s[...]
    term = jnp.sum(term_s[...], axis=1, keepdims=True) * gate * (1.0 - gate) * SCALE
    mine = lanes((SUB, HEAD)) == sublanes((SUB, HEAD))
    for b in range(NBLK):
        rows = slice(b * SUB, (b + 1) * SUB)
        send_ref[b, Q0:G0, :] = dq[rows].astype(BF16)
        across = jnp.sum(jnp.where(mine, term[rows], 0.0), axis=0, keepdims=True)
        send_ref[b, G0:K0, :] = jnp.broadcast_to(across, (16, HEAD)).astype(BF16)


def final_kernel(recv_ref, ghn_ref, gw_ref, dq_ref, dk_ref, dv_ref, dg_ref, dw_ref):
    mine = lanes((SUB, HEAD)) == sublanes((SUB, HEAD))

    def pair(one, two, first, last):
        return recv_ref[one, first:last, :].astype(F32) + recv_ref[two, first:last, :].astype(F32)

    for h in range(HEADS):
        cols = slice(h * HEAD, (h + 1) * HEAD)
        for i in range(2):
            rows = slice(i * SUB, (i + 1) * SUB)
            one, two = device(h, i, 0), device(h, i, 1)
            dq_ref[rows, cols] = pair(one, two, Q0, G0).astype(BF16)
            term = column(pair(one, two, G0, K0)[0:1], mine)
            dg_ref[rows, cols] = (ghn_ref[rows, cols] + term).astype(BF16)
            one, two = device(h, 0, i), device(h, 1, i)
            dk_ref[rows, cols] = pair(one, two, K0, V0).astype(BF16)
            dv_ref[rows, cols] = pair(one, two, V0, PACK).astype(BF16)
    for j in range(D // HEAD):
        dw_ref[:, j * HEAD : (j + 1) * HEAD] = gw_ref[j * 32 : (j + 1) * 32]


VMEM = pl.BlockSpec(memory_space=pltpu.VMEM)
SMEM = pl.BlockSpec(memory_space=pltpu.SMEM)
ANY = pl.BlockSpec(memory_space=pl.ANY)


def call(body, scalars, arrays, outs, scratch=(), us=1.0, space=VMEM, mib=16, after=()):
    if after:
        inner, first = body, len(scalars) + len(arrays)

        def body(*refs):
            inner(*refs[:first], *refs[first + len(after) :])

    moved = sum(x.size * x.dtype.itemsize for x in arrays)
    moved += sum(math.prod(s) * jnp.dtype(t).itemsize for s, t in outs)
    return pl.pallas_call(
        body,
        in_specs=[SMEM] * len(scalars) + [space] * len(arrays) + [ANY] * len(after),
        out_specs=[VMEM] * len(outs),
        out_shape=[jax.ShapeDtypeStruct(s, t) for s, t in outs],
        scratch_shapes=[pltpu.VMEM(*s) if isinstance(s, tuple) else s for s in scratch],
        compiler_params=pltpu.CompilerParams(vmem_limit_bytes=mib * 1024 * 1024),
        cost_estimate=pl.CostEstimate(
            flops=int(us * 1.1e9), bytes_accessed=moved, transcendentals=0
        ),
    )(*scalars, *arrays, *after)


def swap(a, axis):
    return lax.all_to_all(a, axis, 0, 0, tiled=True)


def cross(x, mask):
    return lax.ppermute(x, "dp", [(i, i ^ mask) for i in range(16)])


def pair(x):
    return lax.ppermute(x, "blk", [(i, i ^ 1) for i in range(NBLK)])


def local(q, k, v, u, freqs, w, lens, cot):
    q, k, v, u, cot, lens = q[0], k[0], v[0], u[0], cot[0], lens[0]
    idx = lax.axis_index("blk").astype(jnp.int32)[None]
    staged = [
        ((ROWS, 2 * HEAD), BF16),
        ((ROWS, HEAD), F32),
        ((ROWS, HEAD), F32),
        ((ROWS, HEAD), F32),
    ]
    (send1,) = call(
        pack_kernel,
        [],
        [q, k, v, u],
        [((NBLK, PACK, HEAD), BF16)],
        [((TOK, WIDTH), BF16)] * 4 + [pltpu.SemaphoreType.DMA((4,))],
        space=ANY,
        mib=60,
    )
    recv1 = swap(send1, "blk")
    cot2 = pair(cot)
    (gh,) = call(hidden_grad_kernel, [], [w, cot], [((TOK, WIDTH), F32)])
    mixed, phiq, phik = call(
        forward_kernel,
        [lens, idx],
        [recv1, freqs],
        [((NBLK, SUB, HEAD), BF16), ((ROWS, HEAD), BF16), ((ROWS, HEAD), BF16)],
        staged + [((ROWS, HEAD), F32)],
        after=[gh, cot2],
        us=4.5,
    )
    recv2 = swap(mixed, "blk")
    wide = ((TOK, WIDTH), F32)
    hidden, normed, scales = call(
        norm_kernel,
        [lens, idx],
        [recv2, u],
        [((TOK, WIDTH), BF16), wide, ((TOK, 2 * HEAD), F32)],
        us=0.7,
    )
    hidden2 = pair(hidden)
    scaled, ghn = call(
        scale_kernel, [], [u, gh, normed, scales], [((TOK, WIDTH), BF16), wide], us=0.6
    )
    (send3,) = call(
        weight_kernel,
        [idx],
        [scaled, hidden, hidden2, cot, cot2],
        [((NBLK, SUB + WROWS // 2, HEAD), BF16)],
        us=0.7,
    )
    recv3 = swap(send3, "blk")
    (gw,) = call(sum_kernel, [], [recv3], [((WROWS, HEAD), BF16)])
    (layer_out,) = call(out_kernel, [], [hidden, w], [((TOK, D), BF16)])
    (send4,) = call(
        backward_kernel,
        [lens, idx],
        [recv1, phiq, phik, recv3, freqs],
        [((NBLK, PACK, HEAD), BF16)],
        staged + [((ROWS, HEAD), BF16), ((ROWS, 2 * HEAD), F32), ((ROWS, HEAD), F32)],
        us=5.5,
    )
    (gw,) = call(add_kernel, [], [gw, cross(gw, 8)], [((WROWS, HEAD), BF16)], us=0.5)
    send4, gw = lax.optimization_barrier((send4, gw))
    parts = [gw] + [cross(gw, mask) for mask in (1, 2, 3)]
    (gw,) = call(add_kernel, [], parts, [((WROWS, HEAD), BF16)], us=0.5)
    (gw,) = call(add_kernel, [], [gw, cross(gw, 4)], [((WROWS, HEAD), F32)], us=0.5)
    recv4 = swap(send4, "blk")
    dq, dk, dv, dg, dw = call(
        final_kernel,
        [],
        [recv4, ghn, gw],
        [((TOK, WIDTH), BF16)] * 4 + [((WIDTH // NBLK, D), F32)],
    )
    return layer_out[None], dq[None], dk[None], dv[None], dg[None], dw


def solution(mesh):
    rows = P("dp", "blk", None)
    return jax.shard_map(
        local,
        mesh=mesh,
        in_specs=(rows, rows, rows, rows, P(), P(), P("dp", None), rows),
        out_specs=(rows, rows, rows, rows, rows, P("blk", None)),
        check_vma=False,
    )
```

```python
import math

import jax
import jax.numpy as jnp
from jax import lax
from jax.experimental import pallas as pl
from jax.experimental.pallas import tpu as pltpu
from jax.sharding import PartitionSpec as P

EPS = 1e-05
HEADS, HEAD, FREQS, USERS = 4, 128, 64, 8
TOK, NBLK = 128, 16
SUB = TOK // 2
WIDTH, D = HEADS * HEAD, 1024
ROWS = SUB * NBLK
TILE = 2 * SUB
REACH = 5
TILES = ROWS // TILE
EARLY = 3
SCALE = 1.0 / math.sqrt(HEAD)
F32, BF16 = jnp.float32, jnp.bfloat16

Q0, G0, K0, V0, PACK = 0, SUB, SUB + 16, 2 * SUB + 16, 3 * SUB + 16
WROWS = (WIDTH // NBLK) * D // HEAD


def device(h, gq, gk):
    return 4 * h + 2 * gq + gk


NT = (((1,), (1,)), ((), ()))
NN = (((1,), (0,)), ((), ()))
TN = (((0,), (0,)), ((), ()))


def mm(a, b, dims):
    return lax.dot_general(a, b, dims, preferred_element_type=F32)


def lanes(shape):
    return lax.broadcasted_iota(jnp.int32, shape, 1)


def sublanes(shape):
    return lax.broadcasted_iota(jnp.int32, shape, 0)


def column(row, mine):
    return jnp.sum(jnp.where(mine, row, 0.0), axis=1, keepdims=True)


def starts_of(lens_ref, pos):
    end = jnp.int32(0)
    start = jnp.zeros_like(pos)
    for u in range(USERS):
        end = end + lens_ref[0, u]
        start = jnp.where(pos >= end, end, start)
    return start


def cos_sin(angles):
    turns = jnp.floor(angles * (2.0 / math.pi) + 0.5)
    r = angles - turns * 1.5703125
    r = r - turns * 4.837512969970703125e-4
    r = r - turns * 7.54978995489188e-8
    quad = turns.astype(jnp.int32) - jnp.where(lanes(angles.shape) >= FREQS, 1, 0)
    z = r * r
    c = 1.0 - 0.5 * z + z * z * (4.166664568e-2 + z * (-1.388731625e-3 + z * 2.443315712e-5))
    s = r + r * z * (-1.6666654611e-1 + z * (8.3321608736e-3 - z * 1.9515295891e-4))
    odd = (quad & 1) == 1
    value = jnp.where(odd, s, c)
    return jnp.where(((quad + 1) & 2) == 2, -value, value)


def pack_kernel(q_hbm, k_hbm, v_hbm, u_hbm, out_ref, q_ref, k_ref, v_ref, u_ref, sems):
    pairs = ((u_hbm, u_ref), (q_hbm, q_ref), (k_hbm, k_ref), (v_hbm, v_ref))
    copies = [pltpu.make_async_copy(src, dst, sems.at[i]) for i, (src, dst) in enumerate(pairs)]
    for copy in copies:
        copy.start()
    ones = jnp.ones((16, HEAD), BF16)
    copies[0].wait()
    for h in range(HEADS):
        total = mm(ones, u_ref[:, h * HEAD : (h + 1) * HEAD], NT)
        gate = jax.nn.sigmoid(total * SCALE)
        high = gate.astype(BF16).astype(F32)
        gate = jnp.where(sublanes((16, TOK)) < 8, high, gate - high).astype(BF16)
        for d in range(device(h, 0, 0), device(h, 1, 1) + 1):
            out_ref[d, G0:K0, :] = gate
    for copy in copies[1:]:
        copy.wait()
    for h in range(HEADS):
        cols = slice(h * HEAD, (h + 1) * HEAD)
        for gq in range(2):
            for gk in range(2):
                d = device(h, gq, gk)
                out_ref[d, Q0:G0, :] = q_ref[gq * SUB : (gq + 1) * SUB, cols]
                out_ref[d, K0:V0, :] = k_ref[gk * SUB : (gk + 1) * SUB, cols]
                out_ref[d, V0:PACK, :] = v_ref[gk * SUB : (gk + 1) * SUB, cols]


def stage_rows(recv_ref, lens_ref, gq, gate_s, start_s):
    pos = sublanes((NBLK, TOK)) * TOK + lanes((NBLK, TOK))
    starts = starts_of(lens_ref, pos).astype(F32)
    mine = lanes((SUB, TOK)) == sublanes((SUB, TOK)) + gq * SUB
    for b in range(NBLK):
        rows = slice(b * SUB, (b + 1) * SUB)
        parts = recv_ref[b, G0:K0, :].astype(F32)
        gate_s[rows, :] = jnp.broadcast_to(column(parts[0:1] + parts[8:9], mine), (SUB, HEAD))
        start_s[rows, :] = jnp.broadcast_to(column(starts[b : b + 1], mine), (SUB, HEAD))


def tile_of(recv_ref, c, first, last):
    return jnp.concatenate(
        [recv_ref[2 * c, first:last, :], recv_ref[2 * c + 1, first:last, :]], axis=0
    )


def diagonal(a, b):
    zero = jnp.zeros_like(a)
    return jnp.concatenate(
        [jnp.concatenate([a, zero], axis=1), jnp.concatenate([zero, b], axis=1)], axis=0
    )


def masker(start_s, rows, c, gq, gk):
    lane = lanes((1, TILE))
    key = ((2 * c + (lane >> 6)) * TOK + gk * SUB + (lane & (SUB - 1))).astype(F32)
    row = sublanes((TILE, TILE))
    pos = ((2 * c + (row >> 6)) * TOK + gq * SUB + (row & (SUB - 1))).astype(F32)
    top = slice(rows.start, rows.start + TILE)
    near = (key >= start_s[top, :]) & (key <= pos)
    if rows.stop == top.stop:
        return lambda x: jnp.where(near, x, 0.0)
    far = key >= start_s[top.stop : rows.stop, :]

    def masked(x):
        return jnp.concatenate(
            [jnp.where(near, x[:TILE], 0.0), jnp.where(far, x[TILE:], 0.0)], axis=0
        )

    return masked


def place(idx_ref):
    return idx_ref[0] // 4, (idx_ref[0] // 2) % 2, idx_ref[0] % 2


def tile_rows(c):
    return slice(c * TILE, min(c + REACH, TILES) * TILE)


def forward_kernel(
    idx_ref, recv_ref, freq_ref, lens_hbm, mixed_ref, phik_ref, qp_ref, gate_ref, start_ref,
    acc_s, lens_s, sem,
):
    copy = pltpu.make_async_copy(lens_hbm, lens_s, sem)
    copy.start()
    head, gq, gk = place(idx_ref)
    freq = freq_ref[head]
    freq = jnp.concatenate([freq, freq], axis=1)
    pieces = []
    for _ in range(3):
        piece = freq.astype(BF16)
        pieces.append(piece)
        freq = freq - piece.astype(F32)
    pieces = jnp.concatenate(pieces, axis=1)

    def phi_of(x):
        a = mm(x, pieces, NN)
        angles = (a[:, 2 * HEAD :] + a[:, HEAD : 2 * HEAD]) + a[:, :HEAD]
        return (cos_sin(angles) / math.sqrt(FREQS)).astype(BF16)

    for b in range(NBLK):
        qp_ref[b * SUB : (b + 1) * SUB, :HEAD] = recv_ref[b, Q0:G0, :]
    for i in range(4):
        rows = slice(i * ROWS // 4, (i + 1) * ROWS // 4)
        qp_ref[rows, HEAD:] = phi_of(qp_ref[rows, :HEAD])
    copy.wait()
    stage_rows(recv_ref, lens_s, gq, gate_ref, start_ref)
    acc_s[...] = jnp.zeros_like(acc_s)
    for c in range(TILES):
        rows = tile_rows(c)
        keys = tile_of(recv_ref, c, K0, V0)
        values = tile_of(recv_ref, c, V0, PACK)
        phik = phi_of(keys)
        phik_ref[c * TILE : (c + 1) * TILE, :] = phik
        both = mm(qp_ref[rows, :], diagonal(keys, phik), NT)
        half, kern = both[:, :TILE] * (0.5 * SCALE), both[:, TILE:]
        both = half + half * jnp.tanh(half) + gate_ref[rows, :] * kern
        both = masker(start_ref, rows, c, gq, gk)(both).astype(BF16)
        acc_s[rows, :] += mm(both, values, NN)
    for b in range(NBLK):
        mixed_ref[b] = acc_s[b * SUB : (b + 1) * SUB, :].astype(BF16)


def hidden_grad_kernel(w_ref, cot_ref, gh_ref):
    gh_ref[...] = mm(cot_ref[...], w_ref[...], NT)


def norm_kernel(lens_ref, idx_ref, mixed_ref, u_ref, hid_ref, normed_ref, scales_ref):
    pos = idx_ref[0] * TOK + sublanes((TOK, HEAD))
    count = (pos - starts_of(lens_ref, pos) + 1).astype(F32)
    inverse = jnp.concatenate([1.0 / count] * HEADS, axis=1)
    mixed = []
    for h in range(HEADS):
        halves = [
            mixed_ref[device(h, gq, 0)].astype(F32) + mixed_ref[device(h, gq, 1)].astype(F32)
            for gq in range(2)
        ]
        mixed.append(jnp.concatenate(halves, axis=0))
    mixed = jnp.concatenate(mixed, axis=1) * inverse
    gates = u_ref[...].astype(F32)
    centered = mixed - jnp.mean(mixed, axis=1, keepdims=True)
    rstd = lax.rsqrt(jnp.mean(centered * centered, axis=1, keepdims=True) + EPS)
    normed = centered * rstd
    hid_ref[...] = (normed * gates).astype(BF16)
    normed_ref[...] = normed
    scales_ref[:, :HEAD] = jnp.broadcast_to(rstd, (TOK, HEAD))
    scales_ref[:, HEAD:] = inverse[:, :HEAD]


def scale_kernel(u_ref, gh_ref, normed_ref, scales_ref, scaled_ref, ghn_ref):
    gates, normed, grad_hidden = u_ref[...].astype(F32), normed_ref[...], gh_ref[...]
    rstd = jnp.concatenate([scales_ref[:, :HEAD]] * HEADS, axis=1)
    inverse = jnp.concatenate([scales_ref[:, HEAD:]] * HEADS, axis=1)
    ghn_ref[...] = grad_hidden * normed
    grad_normed = grad_hidden * gates
    grad_mixed = rstd * (
        grad_normed
        - jnp.mean(grad_normed, axis=1, keepdims=True)
        - normed * jnp.mean(grad_normed * normed, axis=1, keepdims=True)
    )
    scaled_ref[...] = (grad_mixed * inverse).astype(BF16)


def weight_kernel(idx_ref, scaled_ref, hid_ref, hid2_ref, cot_ref, cot2_ref, send_ref):
    for h in range(HEADS):
        for gq in range(2):
            for gk in range(2):
                send_ref[device(h, gq, gk), 0:SUB, :] = scaled_ref[
                    gq * SUB : (gq + 1) * SUB, h * HEAD : (h + 1) * HEAD
                ]
    hidden = jnp.concatenate([hid_ref[...], hid2_ref[...]], axis=0)
    first = (idx_ref[0] % 2) * (D // 2)
    for j in range(D // 2 // 256):
        cols = pl.ds(pl.multiple_of(first + j * 256, 256), 256)
        cots = jnp.concatenate([cot_ref[:, cols], cot2_ref[:, cols]], axis=0)
        part = mm(hidden, cots, TN).astype(BF16)
        for i in range(2):
            top = SUB + (2 * j + i) * 32
            for d in range(NBLK):
                send_ref[d, top : top + 32, :] = part[
                    d * 32 : (d + 1) * 32, i * HEAD : (i + 1) * HEAD
                ]


def out_kernel(hid_ref, w_ref, out_ref):
    out_ref[...] = mm(hid_ref[...], w_ref[...], NN).astype(BF16)


def sum_kernel(parts_ref, gw_ref):
    for half in range(2):
        total = parts_ref[half, SUB:, :].astype(F32)
        for d in range(half + 2, NBLK, 2):
            total = total + parts_ref[d, SUB:, :].astype(F32)
        gw_ref[half * WROWS // 2 : (half + 1) * WROWS // 2, :] = total.astype(BF16)


def add_kernel(*refs):
    parts = [ref[...].astype(F32) for ref in refs[:-1]]
    total = parts[0] + parts[1]
    if len(parts) == 4:
        total = total + (parts[2] + parts[3])
    refs[-1][...] = total.astype(refs[-1].dtype)


def backward_tiles(
    tiles, idx_ref, recv_ref, phik_ref, qp_ref, gate_ref, start_ref, sc_ref, freq_ref, out_ref, top,
    dqp_ref, term_ref,
):
    head, gq, gk = place(idx_ref)
    freq = freq_ref[head].astype(BF16)
    freq = jnp.concatenate([freq, -freq], axis=1)

    def feature_back(phi, grad_phi):
        turned = pltpu.roll(grad_phi, FREQS, 1)
        return mm((phi.astype(F32) * turned).astype(BF16), freq, NT)

    for c in tiles:
        rows = tile_rows(c)
        keys = tile_of(recv_ref, c, K0, V0)
        values = tile_of(recv_ref, c, V0, PACK)
        phik = phik_ref[c * TILE : (c + 1) * TILE, :]
        pairs = diagonal(keys, phik)
        scaled, gate = sc_ref[rows, :], gate_ref[rows, :]
        masked = masker(start_ref, rows, c, gq, gk)
        both = mm(qp_ref[rows, :], pairs, NT)
        half, kern = both[:, :TILE] * (0.5 * SCALE), both[:, TILE:]
        t = jnp.tanh(half)
        weights = half + half * t
        slope = (1.0 + t) + weights * (1.0 - t)
        grad_w = masked(mm(scaled, values, NT))
        both = masked(weights + gate * kern).astype(BF16)
        grad_s = (grad_w * slope * (0.5 * SCALE)).astype(BF16)
        grad_k = (grad_w * gate).astype(BF16)
        term_ref[rows, :] += kern * grad_w
        dqp_ref[rows, :] += mm(jnp.concatenate([grad_s, grad_k], axis=1), pairs, NN)
        dkey = mm(grad_s, qp_ref[rows, :HEAD], TN)
        dkey = dkey + feature_back(phik, mm(grad_k, qp_ref[rows, HEAD:], TN))
        dval = mm(both, scaled, TN)
        for i in range(2):
            half = slice(i * SUB, (i + 1) * SUB)
            out_ref[2 * c + i, top : top + SUB, :] = dkey[half].astype(BF16)
            out_ref[2 * c + i, top + SUB : top + 2 * SUB, :] = dval[half].astype(BF16)
    return feature_back


def first_backward_kernel(
    idx_ref, recv_ref, phik_ref, qp_ref, gate_ref, start_ref, grads_ref, freq_ref,
    dkv_ref, sc_ref, dqp_ref, term_ref,
):
    for b in range(NBLK):
        sc_ref[b * SUB : (b + 1) * SUB, :] = grads_ref[b, 0:SUB, :]
    dqp_ref[...] = jnp.zeros_like(dqp_ref)
    term_ref[...] = jnp.zeros_like(term_ref)
    backward_tiles(
        range(EARLY), idx_ref, recv_ref, phik_ref, qp_ref, gate_ref, start_ref, sc_ref, freq_ref,
        dkv_ref, 0, dqp_ref, term_ref,
    )


def second_backward_kernel(
    idx_ref, recv_ref, phik_ref, qp_ref, gate_ref, start_ref, sc_ref, dkv_ref, dqp1_ref, term1_ref,
    freq_ref, send_ref, dqp_s, term_s,
):
    dqp_s[...] = dqp1_ref[...]
    term_s[...] = term1_ref[...]
    feature_back = backward_tiles(
        range(EARLY, TILES), idx_ref, recv_ref, phik_ref, qp_ref, gate_ref, start_ref, sc_ref,
        freq_ref, send_ref, K0, dqp_s, term_s,
    )
    for b in range(2 * EARLY):
        send_ref[b, K0:PACK, :] = dkv_ref[b]
    dq = dqp_s[:, :HEAD] + feature_back(qp_ref[:, HEAD:], dqp_s[:, HEAD:])
    gate = gate_ref[...]
    term = jnp.sum(term_s[...], axis=1, keepdims=True) * gate * (1.0 - gate) * SCALE
    mine = lanes((SUB, HEAD)) == sublanes((SUB, HEAD))
    for b in range(NBLK):
        rows = slice(b * SUB, (b + 1) * SUB)
        send_ref[b, Q0:G0, :] = dq[rows].astype(BF16)
        across = jnp.sum(jnp.where(mine, term[rows], 0.0), axis=0, keepdims=True)
        send_ref[b, G0:K0, :] = jnp.broadcast_to(across, (16, HEAD)).astype(BF16)


def final_kernel(recv_ref, ghn_ref, gw_ref, dq_ref, dk_ref, dv_ref, dg_ref, dw_ref):
    mine = lanes((SUB, HEAD)) == sublanes((SUB, HEAD))

    def pair(one, two, first, last):
        return recv_ref[one, first:last, :].astype(F32) + recv_ref[two, first:last, :].astype(F32)

    for h in range(HEADS):
        cols = slice(h * HEAD, (h + 1) * HEAD)
        for i in range(2):
            rows = slice(i * SUB, (i + 1) * SUB)
            one, two = device(h, i, 0), device(h, i, 1)
            dq_ref[rows, cols] = pair(one, two, Q0, G0).astype(BF16)
            term = column(pair(one, two, G0, K0)[0:1], mine)
            dg_ref[rows, cols] = (ghn_ref[rows, cols] + term).astype(BF16)
            one, two = device(h, 0, i), device(h, 1, i)
            dk_ref[rows, cols] = pair(one, two, K0, V0).astype(BF16)
            dv_ref[rows, cols] = pair(one, two, V0, PACK).astype(BF16)
    for j in range(D // HEAD):
        dw_ref[:, j * HEAD : (j + 1) * HEAD] = gw_ref[j * 32 : (j + 1) * 32]


VMEM = pl.BlockSpec(memory_space=pltpu.VMEM)
SMEM = pl.BlockSpec(memory_space=pltpu.SMEM)
ANY = pl.BlockSpec(memory_space=pl.ANY)


def call(body, scalars, arrays, outs, scratch=(), us=1.0, space=VMEM, to=VMEM, mib=16, after=(), spaces=None):
    if after:
        inner, first = body, len(scalars) + len(arrays)

        def body(*refs):
            inner(*refs[:first], *refs[first + len(after) :])

    moved = sum(x.size * x.dtype.itemsize for x in arrays)
    moved += sum(math.prod(s) * jnp.dtype(t).itemsize for s, t in outs)
    return pl.pallas_call(
        body,
        in_specs=[SMEM] * len(scalars)
        + (spaces or [space] * len(arrays))
        + [ANY] * len(after),
        out_specs=[to] * len(outs),
        out_shape=[jax.ShapeDtypeStruct(s, t) for s, t in outs],
        scratch_shapes=[pltpu.VMEM(*s) if isinstance(s, tuple) else s for s in scratch],
        compiler_params=pltpu.CompilerParams(vmem_limit_bytes=mib * 1024 * 1024),
        cost_estimate=pl.CostEstimate(
            flops=int(us * 1.1e9), bytes_accessed=moved, transcendentals=0
        ),
    )(*scalars, *arrays, *after)


def swap(a, axis):
    return lax.all_to_all(a, axis, 0, 0, tiled=True)


def cross(x, mask):
    return lax.ppermute(x, "dp", [(i, i ^ mask) for i in range(16)])


def pair(x):
    return lax.ppermute(x, "blk", [(i, i ^ 1) for i in range(NBLK)])


def local(q, k, v, u, freqs, w, lens, cot):
    q, k, v, u, cot, lens = q[0], k[0], v[0], u[0], cot[0], lens
    idx = lax.axis_index("blk").astype(jnp.int32)[None]
    rows, tall = (ROWS, HEAD), (ROWS, 2 * HEAD)
    (send1,) = call(
        pack_kernel,
        [],
        [q, k, v, u],
        [((NBLK, PACK, HEAD), BF16)],
        [((TOK, WIDTH), BF16)] * 4 + [pltpu.SemaphoreType.DMA((4,))],
        space=ANY,
        mib=60,
    )
    recv1 = swap(send1, "blk")
    cot2 = pair(cot)
    (gh,) = call(hidden_grad_kernel, [], [w, cot], [((TOK, WIDTH), F32)])
    mixed, phik, qp, gate, start = call(
        forward_kernel,
        [idx],
        [recv1, freqs, lens],
        [((NBLK, SUB, HEAD), BF16), (rows, BF16), (tall, BF16), (rows, F32), (rows, F32)],
        [(rows, F32), pltpu.SMEM((1, USERS), jnp.int32), pltpu.SemaphoreType.DMA(())],
        spaces=[VMEM, VMEM, ANY],
        after=[gh, cot2],
        us=3.5,
    )
    recv2 = swap(mixed, "blk")
    wide = ((TOK, WIDTH), F32)
    hidden, normed, scales = call(
        norm_kernel,
        [lens, idx],
        [recv2, u],
        [((TOK, WIDTH), BF16), wide, ((TOK, 2 * HEAD), F32)],
        us=0.7,
    )
    hidden2 = pair(hidden)
    scaled, ghn = call(
        scale_kernel, [], [u, gh, normed, scales], [((TOK, WIDTH), BF16), wide], us=0.6
    )
    (send3,) = call(
        weight_kernel,
        [idx],
        [scaled, hidden, hidden2, cot, cot2],
        [((NBLK, SUB + WROWS // 2, HEAD), BF16)],
        us=0.7,
    )
    recv3 = swap(send3, "blk")
    (gw,) = call(sum_kernel, [], [recv3], [((WROWS, HEAD), BF16)])
    (layer_out,) = call(out_kernel, [], [hidden, w], [((TOK, D), BF16)])
    shared = [recv1, phik, qp, gate, start]
    dkv, scaled, dqp, term = call(
        first_backward_kernel,
        [idx],
        shared + [recv3, freqs],
        [((2 * EARLY, 2 * SUB, HEAD), BF16), (rows, BF16), (tall, F32), (rows, F32)],
        us=3.0,
    )
    (gw,) = call(
        add_kernel, [], [gw, cross(gw, 8)], [((WROWS, HEAD), BF16)], us=0.5, after=[dkv]
    )
    (send4,) = call(
        second_backward_kernel,
        [idx],
        shared + [scaled, dkv, dqp, term, freqs],
        [((NBLK, PACK, HEAD), BF16)],
        [(tall, F32), (rows, F32)],
        us=3.0,
        after=[gw],
    )
    (gw,) = call(
        add_kernel, [], [gw, cross(gw, 1)], [((WROWS, HEAD), BF16)], us=0.5, after=[send4]
    )
    send4, gw = lax.optimization_barrier((send4, gw))
    parts = [gw] + [cross(gw, mask) for mask in (2, 4, 6)]
    (gw,) = call(add_kernel, [], parts, [((WROWS, HEAD), F32)], us=0.5)
    recv4 = swap(send4, "blk")
    dq, dk, dv, dg, dw = call(
        final_kernel,
        [],
        [recv4, ghn, gw],
        [((TOK, WIDTH), BF16)] * 4 + [((WIDTH // NBLK, D), F32)],
    )
    return layer_out[None], dq[None], dk[None], dv[None], dg[None], dw


def solution(mesh):
    rows = P("dp", "blk", None)
    return jax.shard_map(
        local,
        mesh=mesh,
        in_specs=(rows, rows, rows, rows, P(), P(), P("dp", None), rows),
        out_specs=(rows, rows, rows, rows, rows, P("blk", None)),
        check_vma=False,
    )
```

```python
import math

import jax
import jax.numpy as jnp
from jax import lax
from jax.experimental import pallas as pl
from jax.experimental.pallas import tpu as pltpu
from jax.sharding import PartitionSpec as P

EPS = 1e-05
HEADS, HEAD, FREQS, USERS = 4, 128, 64, 8
TOK, NBLK = 128, 16
SUB = TOK // 2
WIDTH, D = HEADS * HEAD, 1024
ROWS = SUB * NBLK
SPAN = 4
TILE = SPAN * SUB
REACH = 3
TILES = ROWS // TILE
EARLY = 2
SCALE = 1.0 / math.sqrt(HEAD)
F32, BF16 = jnp.float32, jnp.bfloat16

Q0, G0, K0, V0, PACK = 0, SUB, SUB + 16, 2 * SUB + 16, 3 * SUB + 16
WROWS = (WIDTH // NBLK) * D // HEAD


def device(h, gq, gk):
    return 4 * h + 2 * gq + gk


NT = (((1,), (1,)), ((), ()))
NN = (((1,), (0,)), ((), ()))
TN = (((0,), (0,)), ((), ()))


def mm(a, b, dims):
    return lax.dot_general(a, b, dims, preferred_element_type=F32)


def lanes(shape):
    return lax.broadcasted_iota(jnp.int32, shape, 1)


def sublanes(shape):
    return lax.broadcasted_iota(jnp.int32, shape, 0)


def column(row, mine):
    return jnp.sum(jnp.where(mine, row, 0.0), axis=1, keepdims=True)


def starts_of(lens_ref, pos):
    end = jnp.int32(0)
    start = jnp.zeros_like(pos)
    for u in range(USERS):
        end = end + lens_ref[0, u]
        start = jnp.where(pos >= end, end, start)
    return start


def cos_sin(angles):
    turns = jnp.floor(angles * (2.0 / math.pi) + 0.5)
    r = angles - turns * 1.5703125
    r = r - turns * 4.837512969970703125e-4
    r = r - turns * 7.54978995489188e-8
    quad = turns.astype(jnp.int32)
    z = r * r
    c = 1.0 - 0.5 * z + z * z * (4.166664568e-2 + z * (-1.388731625e-3 + z * 2.443315712e-5))
    s = r + r * z * (-1.6666654611e-1 + z * (8.3321608736e-3 - z * 1.9515295891e-4))
    odd = (quad & 1) == 1
    cos, sin = jnp.where(odd, s, c), jnp.where(odd, c, s)
    cos = jnp.where(((quad + 1) & 2) == 2, -cos, cos)
    return cos, jnp.where((quad & 2) == 2, -sin, sin)


def pack_kernel(q_hbm, k_hbm, v_hbm, u_hbm, out_ref, q_ref, k_ref, v_ref, u_ref, sems):
    pairs = ((u_hbm, u_ref), (q_hbm, q_ref), (k_hbm, k_ref), (v_hbm, v_ref))
    copies = [pltpu.make_async_copy(src, dst, sems.at[i]) for i, (src, dst) in enumerate(pairs)]
    for copy in copies:
        copy.start()
    ones = jnp.ones((16, HEAD), BF16)
    copies[0].wait()
    for h in range(HEADS):
        total = mm(ones, u_ref[:, h * HEAD : (h + 1) * HEAD], NT)
        gate = jax.nn.sigmoid(total * SCALE)
        high = gate.astype(BF16).astype(F32)
        gate = jnp.where(sublanes((16, TOK)) < 8, high, gate - high).astype(BF16)
        for d in range(device(h, 0, 0), device(h, 1, 1) + 1):
            out_ref[d, G0:K0, :] = gate
    for copy in copies[1:]:
        copy.wait()
    for h in range(HEADS):
        cols = slice(h * HEAD, (h + 1) * HEAD)
        for gq in range(2):
            for gk in range(2):
                d = device(h, gq, gk)
                out_ref[d, Q0:G0, :] = q_ref[gq * SUB : (gq + 1) * SUB, cols]
                out_ref[d, K0:V0, :] = k_ref[gk * SUB : (gk + 1) * SUB, cols]
                out_ref[d, V0:PACK, :] = v_ref[gk * SUB : (gk + 1) * SUB, cols]


def stage_rows(recv_ref, lens_ref, gq, gate_s, start_s):
    pos = sublanes((NBLK, TOK)) * TOK + lanes((NBLK, TOK))
    starts = starts_of(lens_ref, pos).astype(F32)
    mine = lanes((SUB, TOK)) == sublanes((SUB, TOK)) + gq * SUB
    for b in range(NBLK):
        rows = slice(b * SUB, (b + 1) * SUB)
        parts = recv_ref[b, G0:K0, :].astype(F32)
        gate_s[rows, :] = jnp.broadcast_to(column(parts[0:1] + parts[8:9], mine), (SUB, HEAD))
        start_s[rows, :] = jnp.broadcast_to(column(starts[b : b + 1], mine), (SUB, HEAD))


def tile_of(recv_ref, c, first, last):
    return jnp.concatenate(
        [recv_ref[SPAN * c + i, first:last, :] for i in range(SPAN)], axis=0
    )


def twice(a):
    return jnp.concatenate([a, a], axis=1)


def diagonal(a, b):
    zero = jnp.zeros_like(a)
    return jnp.concatenate(
        [jnp.concatenate([a, zero], axis=1), jnp.concatenate([zero, b], axis=1)], axis=0
    )


def masker(start_s, rows, c, gq, gk):
    lane = lanes((1, TILE))
    key = ((SPAN * c + (lane >> 6)) * TOK + gk * SUB + (lane & (SUB - 1))).astype(F32)
    row = sublanes((TILE, TILE))
    pos = ((SPAN * c + (row >> 6)) * TOK + gq * SUB + (row & (SUB - 1))).astype(F32)
    top = slice(rows.start, rows.start + TILE)
    near = (key >= twice(start_s[top, :])) & (key <= pos)
    if rows.stop == top.stop:
        return lambda x: jnp.where(near, x, 0.0)
    far = key >= twice(start_s[top.stop : rows.stop, :])

    def masked(x):
        return jnp.concatenate(
            [jnp.where(near, x[:TILE], 0.0), jnp.where(far, x[TILE:], 0.0)], axis=0
        )

    return masked


def place(idx_ref):
    return idx_ref[0] // 4, (idx_ref[0] // 2) % 2, idx_ref[0] % 2


def tile_rows(c):
    return slice(c * TILE, min(c + REACH, TILES) * TILE)


def forward_kernel(
    idx_ref, recv_ref, freq_ref, lens_hbm, mixed_ref, phik_ref, qp_ref, gate_ref, start_ref,
    acc_s, lens_s, sem,
):
    copy = pltpu.make_async_copy(lens_hbm, lens_s, sem)
    copy.start()
    head, gq, gk = place(idx_ref)
    freq = freq_ref[head]
    pieces = []
    for _ in range(3):
        piece = freq.astype(BF16)
        pieces.append(diagonal(piece, piece))
        freq = freq - piece.astype(F32)

    def phi_of(x):
        n = x.shape[0] // 2
        x = jnp.concatenate([x[:n], x[n:]], axis=1)
        angles = (mm(x, pieces[2], NN) + mm(x, pieces[1], NN)) + mm(x, pieces[0], NN)
        cos, sin = cos_sin(angles)
        left = lanes((n, HEAD)) < FREQS
        first = jnp.where(left, cos, pltpu.roll(sin, FREQS, 1))
        second = jnp.where(left, pltpu.roll(cos, FREQS, 1), sin)
        return (jnp.concatenate([first, second], axis=0) / math.sqrt(FREQS)).astype(BF16)

    for b in range(NBLK):
        qp_ref[b * SUB : (b + 1) * SUB, :HEAD] = recv_ref[b, Q0:G0, :]
    for i in range(4):
        rows = slice(i * ROWS // 4, (i + 1) * ROWS // 4)
        qp_ref[rows, HEAD:] = phi_of(qp_ref[rows, :HEAD])
    copy.wait()
    stage_rows(recv_ref, lens_s, gq, gate_ref, start_ref)
    acc_s[...] = jnp.zeros_like(acc_s)
    for c in range(TILES):
        rows = tile_rows(c)
        keys = tile_of(recv_ref, c, K0, V0)
        values = tile_of(recv_ref, c, V0, PACK)
        phik = phi_of(keys)
        phik_ref[c * TILE : (c + 1) * TILE, :] = phik
        both = mm(qp_ref[rows, :], diagonal(keys, phik), NT)
        half, kern = both[:, :TILE] * (0.5 * SCALE), both[:, TILE:]
        both = half + half * jnp.tanh(half) + twice(gate_ref[rows, :]) * kern
        both = masker(start_ref, rows, c, gq, gk)(both).astype(BF16)
        acc_s[rows, :] += mm(both, values, NN)
    for b in range(NBLK):
        mixed_ref[b] = acc_s[b * SUB : (b + 1) * SUB, :].astype(BF16)


def hidden_grad_kernel(w_ref, cot_ref, gh_ref):
    gh_ref[...] = mm(cot_ref[...], w_ref[...], NT)


def norm_kernel(lens_ref, idx_ref, mixed_ref, u_ref, hid_ref, normed_ref, scales_ref):
    pos = idx_ref[0] * TOK + sublanes((TOK, HEAD))
    count = (pos - starts_of(lens_ref, pos) + 1).astype(F32)
    inverse = jnp.concatenate([1.0 / count] * HEADS, axis=1)
    mixed = []
    for h in range(HEADS):
        halves = [
            mixed_ref[device(h, gq, 0)].astype(F32) + mixed_ref[device(h, gq, 1)].astype(F32)
            for gq in range(2)
        ]
        mixed.append(jnp.concatenate(halves, axis=0))
    mixed = jnp.concatenate(mixed, axis=1) * inverse
    gates = u_ref[...].astype(F32)
    centered = mixed - jnp.mean(mixed, axis=1, keepdims=True)
    rstd = lax.rsqrt(jnp.mean(centered * centered, axis=1, keepdims=True) + EPS)
    normed = centered * rstd
    hid_ref[...] = (normed * gates).astype(BF16)
    normed_ref[...] = normed
    scales_ref[:, :HEAD] = jnp.broadcast_to(rstd, (TOK, HEAD))
    scales_ref[:, HEAD:] = inverse[:, :HEAD]


def scale_kernel(u_ref, gh_ref, normed_ref, scales_ref, scaled_ref, ghn_ref):
    gates, normed, grad_hidden = u_ref[...].astype(F32), normed_ref[...], gh_ref[...]
    rstd = jnp.concatenate([scales_ref[:, :HEAD]] * HEADS, axis=1)
    inverse = jnp.concatenate([scales_ref[:, HEAD:]] * HEADS, axis=1)
    ghn_ref[...] = grad_hidden * normed
    grad_normed = grad_hidden * gates
    grad_mixed = rstd * (
        grad_normed
        - jnp.mean(grad_normed, axis=1, keepdims=True)
        - normed * jnp.mean(grad_normed * normed, axis=1, keepdims=True)
    )
    scaled_ref[...] = (grad_mixed * inverse).astype(BF16)


def weight_kernel(idx_ref, scaled_ref, hid_ref, hid2_ref, cot_ref, cot2_ref, send_ref):
    for h in range(HEADS):
        for gq in range(2):
            for gk in range(2):
                send_ref[device(h, gq, gk), 0:SUB, :] = scaled_ref[
                    gq * SUB : (gq + 1) * SUB, h * HEAD : (h + 1) * HEAD
                ]
    hidden = jnp.concatenate([hid_ref[...], hid2_ref[...]], axis=0)
    first = (idx_ref[0] % 2) * (D // 2)
    for j in range(D // 2 // 256):
        cols = pl.ds(pl.multiple_of(first + j * 256, 256), 256)
        cots = jnp.concatenate([cot_ref[:, cols], cot2_ref[:, cols]], axis=0)
        part = mm(hidden, cots, TN).astype(BF16)
        for i in range(2):
            top = SUB + (2 * j + i) * 32
            for d in range(NBLK):
                send_ref[d, top : top + 32, :] = part[
                    d * 32 : (d + 1) * 32, i * HEAD : (i + 1) * HEAD
                ]


def out_kernel(hid_ref, w_ref, out_ref):
    out_ref[...] = mm(hid_ref[...], w_ref[...], NN).astype(BF16)


def sum_kernel(parts_ref, gw_ref):
    for half in range(2):
        total = parts_ref[half, SUB:, :].astype(F32)
        for d in range(half + 2, NBLK, 2):
            total = total + parts_ref[d, SUB:, :].astype(F32)
        gw_ref[half * WROWS // 2 : (half + 1) * WROWS // 2, :] = total.astype(BF16)


def add_kernel(*refs):
    parts = [ref[...].astype(F32) for ref in refs[:-1]]
    total = parts[0] + parts[1]
    if len(parts) == 4:
        total = total + (parts[2] + parts[3])
    refs[-1][...] = total.astype(refs[-1].dtype)


def backward_tiles(
    tiles, idx_ref, recv_ref, phik_ref, qp_ref, gate_ref, start_ref, sc_ref, freq_ref, out_ref, top,
    dqp_ref, term_ref,
):
    head, gq, gk = place(idx_ref)
    freq = freq_ref[head].astype(BF16)
    freq = jnp.concatenate([freq, -freq], axis=1)

    def feature_back(phi, grad_phi):
        turned = pltpu.roll(grad_phi, FREQS, 1)
        return mm((phi.astype(F32) * turned).astype(BF16), freq, NT)

    for c in tiles:
        rows = tile_rows(c)
        keys = tile_of(recv_ref, c, K0, V0)
        values = tile_of(recv_ref, c, V0, PACK)
        phik = phik_ref[c * TILE : (c + 1) * TILE, :]
        pairs = diagonal(keys, phik)
        scaled, gate = sc_ref[rows, :], twice(gate_ref[rows, :])
        masked = masker(start_ref, rows, c, gq, gk)
        both = mm(qp_ref[rows, :], pairs, NT)
        half, kern = both[:, :TILE] * (0.5 * SCALE), both[:, TILE:]
        t = jnp.tanh(half)
        weights = half + half * t
        slope = (1.0 + t) + weights * (1.0 - t)
        grad_w = masked(mm(scaled, values, NT))
        both = masked(weights + gate * kern).astype(BF16)
        grad_s = (grad_w * slope * (0.5 * SCALE)).astype(BF16)
        grad_k = (grad_w * gate).astype(BF16)
        term = kern * grad_w
        term_ref[rows, :] += term[:, :HEAD] + term[:, HEAD:]
        dqp_ref[rows, :] += mm(jnp.concatenate([grad_s, grad_k], axis=1), pairs, NN)
        dkey = mm(grad_s, qp_ref[rows, :HEAD], TN)
        dkey = dkey + feature_back(phik, mm(grad_k, qp_ref[rows, HEAD:], TN))
        dval = mm(both, scaled, TN)
        for i in range(SPAN):
            part, b = slice(i * SUB, (i + 1) * SUB), SPAN * c + i
            out_ref[b, top : top + SUB, :] = dkey[part].astype(BF16)
            out_ref[b, top + SUB : top + 2 * SUB, :] = dval[part].astype(BF16)
    return feature_back


def first_backward_kernel(
    idx_ref, recv_ref, phik_ref, qp_ref, gate_ref, start_ref, grads_ref, freq_ref,
    dkv_ref, sc_ref, dqp_ref, term_ref,
):
    for b in range(NBLK):
        sc_ref[b * SUB : (b + 1) * SUB, :] = grads_ref[b, 0:SUB, :]
    dqp_ref[...] = jnp.zeros_like(dqp_ref)
    term_ref[...] = jnp.zeros_like(term_ref)
    backward_tiles(
        range(EARLY), idx_ref, recv_ref, phik_ref, qp_ref, gate_ref, start_ref, sc_ref, freq_ref,
        dkv_ref, 0, dqp_ref, term_ref,
    )


def second_backward_kernel(
    idx_ref, recv_ref, phik_ref, qp_ref, gate_ref, start_ref, sc_ref, dkv_ref, dqp1_ref, term1_ref,
    freq_ref, send_ref, dqp_s, term_s,
):
    dqp_s[...] = dqp1_ref[...]
    term_s[...] = term1_ref[...]
    feature_back = backward_tiles(
        range(EARLY, TILES), idx_ref, recv_ref, phik_ref, qp_ref, gate_ref, start_ref, sc_ref,
        freq_ref, send_ref, K0, dqp_s, term_s,
    )
    for b in range(SPAN * EARLY):
        send_ref[b, K0:PACK, :] = dkv_ref[b]
    dq = dqp_s[:, :HEAD] + feature_back(qp_ref[:, HEAD:], dqp_s[:, HEAD:])
    gate = gate_ref[...]
    term = jnp.sum(term_s[...], axis=1, keepdims=True) * gate * (1.0 - gate) * SCALE
    mine = lanes((SUB, HEAD)) == sublanes((SUB, HEAD))
    for b in range(NBLK):
        rows = slice(b * SUB, (b + 1) * SUB)
        send_ref[b, Q0:G0, :] = dq[rows].astype(BF16)
        across = jnp.sum(jnp.where(mine, term[rows], 0.0), axis=0, keepdims=True)
        send_ref[b, G0:K0, :] = jnp.broadcast_to(across, (16, HEAD)).astype(BF16)


def final_kernel(recv_ref, ghn_ref, gw_ref, dq_ref, dk_ref, dv_ref, dg_ref, dw_ref):
    mine = lanes((SUB, HEAD)) == sublanes((SUB, HEAD))

    def pair(one, two, first, last):
        return recv_ref[one, first:last, :].astype(F32) + recv_ref[two, first:last, :].astype(F32)

    for h in range(HEADS):
        cols = slice(h * HEAD, (h + 1) * HEAD)
        for i in range(2):
            rows = slice(i * SUB, (i + 1) * SUB)
            one, two = device(h, i, 0), device(h, i, 1)
            dq_ref[rows, cols] = pair(one, two, Q0, G0).astype(BF16)
            term = column(pair(one, two, G0, K0)[0:1], mine)
            dg_ref[rows, cols] = (ghn_ref[rows, cols] + term).astype(BF16)
            one, two = device(h, 0, i), device(h, 1, i)
            dk_ref[rows, cols] = pair(one, two, K0, V0).astype(BF16)
            dv_ref[rows, cols] = pair(one, two, V0, PACK).astype(BF16)
    for j in range(D // HEAD):
        dw_ref[:, j * HEAD : (j + 1) * HEAD] = gw_ref[j * 32 : (j + 1) * 32]


VMEM = pl.BlockSpec(memory_space=pltpu.VMEM)
SMEM = pl.BlockSpec(memory_space=pltpu.SMEM)
ANY = pl.BlockSpec(memory_space=pl.ANY)


def call(body, scalars, arrays, outs, scratch=(), us=1.0, space=VMEM, to=VMEM, mib=16, after=(), spaces=None):
    if after:
        inner, first = body, len(scalars) + len(arrays)

        def body(*refs):
            inner(*refs[:first], *refs[first + len(after) :])

    moved = sum(x.size * x.dtype.itemsize for x in arrays)
    moved += sum(math.prod(s) * jnp.dtype(t).itemsize for s, t in outs)
    return pl.pallas_call(
        body,
        in_specs=[SMEM] * len(scalars)
        + (spaces or [space] * len(arrays))
        + [ANY] * len(after),
        out_specs=[to] * len(outs),
        out_shape=[jax.ShapeDtypeStruct(s, t) for s, t in outs],
        scratch_shapes=[pltpu.VMEM(*s) if isinstance(s, tuple) else s for s in scratch],
        compiler_params=pltpu.CompilerParams(vmem_limit_bytes=mib * 1024 * 1024),
        cost_estimate=pl.CostEstimate(
            flops=int(us * 1.1e9), bytes_accessed=moved, transcendentals=0
        ),
    )(*scalars, *arrays, *after)


def swap(a, axis):
    return lax.all_to_all(a, axis, 0, 0, tiled=True)


def cross(x, mask):
    return lax.ppermute(x, "dp", [(i, i ^ mask) for i in range(16)])


def pair(x):
    return lax.ppermute(x, "blk", [(i, i ^ 1) for i in range(NBLK)])


def local(q, k, v, u, freqs, w, lens, cot):
    q, k, v, u, cot, lens = q[0], k[0], v[0], u[0], cot[0], lens
    idx = lax.axis_index("blk").astype(jnp.int32)[None]
    rows, tall = (ROWS, HEAD), (ROWS, 2 * HEAD)
    (send1,) = call(
        pack_kernel,
        [],
        [q, k, v, u],
        [((NBLK, PACK, HEAD), BF16)],
        [((TOK, WIDTH), BF16)] * 4 + [pltpu.SemaphoreType.DMA((4,))],
        space=ANY,
        mib=60,
    )
    recv1 = swap(send1, "blk")
    cot2 = pair(cot)
    (gh,) = call(hidden_grad_kernel, [], [w, cot], [((TOK, WIDTH), F32)])
    mixed, phik, qp, gate, start = call(
        forward_kernel,
        [idx],
        [recv1, freqs, lens],
        [((NBLK, SUB, HEAD), BF16), (rows, BF16), (tall, BF16), (rows, F32), (rows, F32)],
        [(rows, F32), pltpu.SMEM((1, USERS), jnp.int32), pltpu.SemaphoreType.DMA(())],
        spaces=[VMEM, VMEM, ANY],
        after=[gh, cot2],
        us=3.5,
    )
    recv2 = swap(mixed, "blk")
    wide = ((TOK, WIDTH), F32)
    hidden, normed, scales = call(
        norm_kernel,
        [lens, idx],
        [recv2, u],
        [((TOK, WIDTH), BF16), wide, ((TOK, 2 * HEAD), F32)],
        us=0.7,
    )
    hidden2 = pair(hidden)
    scaled, ghn = call(
        scale_kernel, [], [u, gh, normed, scales], [((TOK, WIDTH), BF16), wide], us=0.6
    )
    (send3,) = call(
        weight_kernel,
        [idx],
        [scaled, hidden, hidden2, cot, cot2],
        [((NBLK, SUB + WROWS // 2, HEAD), BF16)],
        us=0.7,
    )
    recv3 = swap(send3, "blk")
    (gw,) = call(sum_kernel, [], [recv3], [((WROWS, HEAD), BF16)])
    (layer_out,) = call(out_kernel, [], [hidden, w], [((TOK, D), BF16)])
    shared = [recv1, phik, qp, gate, start]
    dkv, scaled, dqp, term = call(
        first_backward_kernel,
        [idx],
        shared + [recv3, freqs],
        [((SPAN * EARLY, 2 * SUB, HEAD), BF16), (rows, BF16), (tall, F32), (rows, F32)],
        us=3.0,
    )
    (gw,) = call(
        add_kernel, [], [gw, cross(gw, 8)], [((WROWS, HEAD), BF16)], us=0.5, after=[dkv]
    )
    (send4,) = call(
        second_backward_kernel,
        [idx],
        shared + [scaled, dkv, dqp, term, freqs],
        [((NBLK, PACK, HEAD), BF16)],
        [(tall, F32), (rows, F32)],
        us=3.0,
        after=[gw],
    )
    (gw,) = call(
        add_kernel, [], [gw, cross(gw, 1)], [((WROWS, HEAD), BF16)], us=0.5, after=[send4]
    )
    send4, gw = lax.optimization_barrier((send4, gw))
    parts = [gw] + [cross(gw, mask) for mask in (2, 4, 6)]
    (gw,) = call(add_kernel, [], parts, [((WROWS, HEAD), F32)], us=0.5)
    recv4 = swap(send4, "blk")
    dq, dk, dv, dg, dw = call(
        final_kernel,
        [],
        [recv4, ghn, gw],
        [((TOK, WIDTH), BF16)] * 4 + [((WIDTH // NBLK, D), F32)],
    )
    return layer_out[None], dq[None], dk[None], dv[None], dg[None], dw


def solution(mesh):
    rows = P("dp", "blk", None)
    return jax.shard_map(
        local,
        mesh=mesh,
        in_specs=(rows, rows, rows, rows, P(), P(), P("dp", None), rows),
        out_specs=(rows, rows, rows, rows, rows, P("blk", None)),
        check_vma=False,
    )
```

```python
import math

import jax
import jax.numpy as jnp
from jax import lax
from jax.experimental import pallas as pl
from jax.experimental.pallas import tpu as pltpu
from jax.sharding import PartitionSpec as P

EPS = 1e-05
HEADS, HEAD, FREQS, USERS = 4, 128, 64, 8
TOK, NBLK = 128, 16
SUB = TOK // 2
WIDTH, D = HEADS * HEAD, 1024
ROWS = SUB * NBLK
SPAN = 4
TILE = SPAN * SUB
REACH = 3
TILES = ROWS // TILE
EARLY = 2
SCALE = 1.0 / math.sqrt(HEAD)
F32, BF16 = jnp.float32, jnp.bfloat16

Q0, G0, K0, V0, PACK = 0, SUB, SUB + 16, 2 * SUB + 16, 3 * SUB + 16
WROWS = (WIDTH // NBLK) * D // HEAD


def device(h, gq, gk):
    return 4 * h + 2 * gq + gk


NT = (((1,), (1,)), ((), ()))
NN = (((1,), (0,)), ((), ()))
TN = (((0,), (0,)), ((), ()))


def mm(a, b, dims):
    return lax.dot_general(a, b, dims, preferred_element_type=F32)


def lanes(shape):
    return lax.broadcasted_iota(jnp.int32, shape, 1)


def sublanes(shape):
    return lax.broadcasted_iota(jnp.int32, shape, 0)


def column(row, mine):
    return jnp.sum(jnp.where(mine, row, 0.0), axis=1, keepdims=True)


def starts_of(lens_ref, pos):
    end = jnp.int32(0)
    start = jnp.zeros_like(pos)
    for u in range(USERS):
        end = end + lens_ref[0, u]
        start = jnp.where(pos >= end, end, start)
    return start


def cos_sin(angles):
    turns = jnp.floor(angles * (2.0 / math.pi) + 0.5)
    r = angles - turns * 1.5703125
    r = r - turns * 4.837512969970703125e-4
    r = r - turns * 7.54978995489188e-8
    quad = turns.astype(jnp.int32)
    z = r * r
    c = 1.0 - 0.5 * z + z * z * (4.166664568e-2 + z * (-1.388731625e-3 + z * 2.443315712e-5))
    s = r + r * z * (-1.6666654611e-1 + z * (8.3321608736e-3 - z * 1.9515295891e-4))
    odd = (quad & 1) == 1
    cos, sin = jnp.where(odd, s, c), jnp.where(odd, c, s)
    cos = jnp.where(((quad + 1) & 2) == 2, -cos, cos)
    return cos, jnp.where((quad & 2) == 2, -sin, sin)


def pack_kernel(q_hbm, k_hbm, v_hbm, u_hbm, out_ref, q_ref, k_ref, v_ref, u_ref, sems):
    pairs = ((u_hbm, u_ref), (q_hbm, q_ref), (k_hbm, k_ref), (v_hbm, v_ref))
    copies = [pltpu.make_async_copy(src, dst, sems.at[i]) for i, (src, dst) in enumerate(pairs)]
    for copy in copies:
        copy.start()
    ones = jnp.ones((16, HEAD), BF16)
    copies[0].wait()
    for h in range(HEADS):
        total = mm(ones, u_ref[:, h * HEAD : (h + 1) * HEAD], NT)
        gate = jax.nn.sigmoid(total * SCALE)
        high = gate.astype(BF16).astype(F32)
        gate = jnp.where(sublanes((16, TOK)) < 8, high, gate - high).astype(BF16)
        for d in range(device(h, 0, 0), device(h, 1, 1) + 1):
            out_ref[d, G0:K0, :] = gate
    for copy in copies[1:]:
        copy.wait()
    for h in range(HEADS):
        cols = slice(h * HEAD, (h + 1) * HEAD)
        for gq in range(2):
            for gk in range(2):
                d = device(h, gq, gk)
                out_ref[d, Q0:G0, :] = q_ref[gq * SUB : (gq + 1) * SUB, cols]
                out_ref[d, K0:V0, :] = k_ref[gk * SUB : (gk + 1) * SUB, cols]
                out_ref[d, V0:PACK, :] = v_ref[gk * SUB : (gk + 1) * SUB, cols]


def stage_rows(recv_ref, lens_ref, gq, gate_s, start_s):
    pos = sublanes((NBLK, TOK)) * TOK + lanes((NBLK, TOK))
    starts = starts_of(lens_ref, pos).astype(F32)
    mine = lanes((SUB, TOK)) == sublanes((SUB, TOK)) + gq * SUB
    for b in range(NBLK):
        rows = slice(b * SUB, (b + 1) * SUB)
        parts = recv_ref[b, G0:K0, :].astype(F32)
        gate_s[rows, :] = jnp.broadcast_to(column(parts[0:1] + parts[8:9], mine), (SUB, HEAD))
        start_s[rows, :] = jnp.broadcast_to(column(starts[b : b + 1], mine), (SUB, HEAD))


def tile_of(recv_ref, c, first, last):
    return jnp.concatenate(
        [recv_ref[SPAN * c + i, first:last, :] for i in range(SPAN)], axis=0
    )


def twice(a):
    return jnp.concatenate([a, a], axis=1)


def diagonal(a, b):
    zero = jnp.zeros_like(a)
    return jnp.concatenate(
        [jnp.concatenate([a, zero], axis=1), jnp.concatenate([zero, b], axis=1)], axis=0
    )


def masker(start_s, rows, c, gq, gk):
    lane = lanes((1, TILE))
    key = ((SPAN * c + (lane >> 6)) * TOK + gk * SUB + (lane & (SUB - 1))).astype(F32)
    row = sublanes((TILE, TILE))
    pos = ((SPAN * c + (row >> 6)) * TOK + gq * SUB + (row & (SUB - 1))).astype(F32)
    top = slice(rows.start, rows.start + TILE)
    near = (key >= twice(start_s[top, :])) & (key <= pos)
    if rows.stop == top.stop:
        return lambda x: jnp.where(near, x, 0.0)
    far = key >= twice(start_s[top.stop : rows.stop, :])

    def masked(x):
        return jnp.concatenate(
            [jnp.where(near, x[:TILE], 0.0), jnp.where(far, x[TILE:], 0.0)], axis=0
        )

    return masked


def place(idx_ref):
    return idx_ref[0] // 4, (idx_ref[0] // 2) % 2, idx_ref[0] % 2


def tile_rows(c):
    return slice(c * TILE, min(c + REACH, TILES) * TILE)


def forward_kernel(
    idx_ref, recv_ref, freq_ref, lens_hbm, mixed_ref, phik_ref, qp_ref, gate_ref, start_ref,
    acc_s, lens_s, sem,
):
    copy = pltpu.make_async_copy(lens_hbm, lens_s, sem)
    copy.start()
    head, gq, gk = place(idx_ref)
    freq = freq_ref[head]
    pieces = []
    for _ in range(3):
        piece = freq.astype(BF16)
        pieces.append(diagonal(piece, piece))
        freq = freq - piece.astype(F32)

    def phi_of(x):
        n = x.shape[0] // 2
        x = jnp.concatenate([x[:n], x[n:]], axis=1)
        angles = (mm(x, pieces[2], NN) + mm(x, pieces[1], NN)) + mm(x, pieces[0], NN)
        cos, sin = cos_sin(angles)
        left = lanes((n, HEAD)) < FREQS
        first = jnp.where(left, cos, pltpu.roll(sin, FREQS, 1))
        second = jnp.where(left, pltpu.roll(cos, FREQS, 1), sin)
        return (jnp.concatenate([first, second], axis=0) / math.sqrt(FREQS)).astype(BF16)

    for b in range(NBLK):
        qp_ref[b * SUB : (b + 1) * SUB, :HEAD] = recv_ref[b, Q0:G0, :]
    qp_ref[:, HEAD:] = phi_of(qp_ref[:, :HEAD])
    phik_ref[...] = phi_of(
        jnp.concatenate([recv_ref[b, K0:V0, :] for b in range(NBLK)], axis=0)
    )
    copy.wait()
    stage_rows(recv_ref, lens_s, gq, gate_ref, start_ref)
    acc_s[...] = jnp.zeros_like(acc_s)
    for c in range(TILES):
        rows = tile_rows(c)
        keys = tile_of(recv_ref, c, K0, V0)
        values = tile_of(recv_ref, c, V0, PACK)
        phik = phik_ref[c * TILE : (c + 1) * TILE, :]
        both = mm(qp_ref[rows, :], diagonal(keys, phik), NT)
        half, kern = both[:, :TILE] * (0.5 * SCALE), both[:, TILE:]
        both = half + half * jnp.tanh(half) + twice(gate_ref[rows, :]) * kern
        both = masker(start_ref, rows, c, gq, gk)(both).astype(BF16)
        acc_s[rows, :] += mm(both, values, NN)
    for b in range(NBLK):
        mixed_ref[b] = acc_s[b * SUB : (b + 1) * SUB, :].astype(BF16)


def hidden_grad_kernel(w_ref, cot_ref, gh_ref):
    gh_ref[...] = mm(cot_ref[...], w_ref[...], NT)


def norm_kernel(lens_ref, idx_ref, mixed_ref, u_ref, hid_ref, normed_ref, scales_ref):
    pos = idx_ref[0] * TOK + sublanes((TOK, HEAD))
    count = (pos - starts_of(lens_ref, pos) + 1).astype(F32)
    inverse = jnp.concatenate([1.0 / count] * HEADS, axis=1)
    mixed = []
    for h in range(HEADS):
        halves = [
            mixed_ref[device(h, gq, 0)].astype(F32) + mixed_ref[device(h, gq, 1)].astype(F32)
            for gq in range(2)
        ]
        mixed.append(jnp.concatenate(halves, axis=0))
    mixed = jnp.concatenate(mixed, axis=1) * inverse
    gates = u_ref[...].astype(F32)
    centered = mixed - jnp.mean(mixed, axis=1, keepdims=True)
    rstd = lax.rsqrt(jnp.mean(centered * centered, axis=1, keepdims=True) + EPS)
    normed = centered * rstd
    hid_ref[...] = (normed * gates).astype(BF16)
    normed_ref[...] = normed
    scales_ref[:, :HEAD] = jnp.broadcast_to(rstd, (TOK, HEAD))
    scales_ref[:, HEAD:] = inverse[:, :HEAD]


def scale_kernel(u_ref, gh_ref, normed_ref, scales_ref, scaled_ref, ghn_ref):
    gates, normed, grad_hidden = u_ref[...].astype(F32), normed_ref[...], gh_ref[...]
    rstd = jnp.concatenate([scales_ref[:, :HEAD]] * HEADS, axis=1)
    inverse = jnp.concatenate([scales_ref[:, HEAD:]] * HEADS, axis=1)
    ghn_ref[...] = grad_hidden * normed
    grad_normed = grad_hidden * gates
    grad_mixed = rstd * (
        grad_normed
        - jnp.mean(grad_normed, axis=1, keepdims=True)
        - normed * jnp.mean(grad_normed * normed, axis=1, keepdims=True)
    )
    scaled_ref[...] = (grad_mixed * inverse).astype(BF16)


def weight_kernel(idx_ref, scaled_ref, hid_ref, hid2_ref, cot_ref, cot2_ref, send_ref):
    for h in range(HEADS):
        for gq in range(2):
            for gk in range(2):
                send_ref[device(h, gq, gk), 0:SUB, :] = scaled_ref[
                    gq * SUB : (gq + 1) * SUB, h * HEAD : (h + 1) * HEAD
                ]
    hidden = jnp.concatenate([hid_ref[...], hid2_ref[...]], axis=0)
    first = (idx_ref[0] % 2) * (D // 2)
    for j in range(D // 2 // 256):
        cols = pl.ds(pl.multiple_of(first + j * 256, 256), 256)
        cots = jnp.concatenate([cot_ref[:, cols], cot2_ref[:, cols]], axis=0)
        part = mm(hidden, cots, TN).astype(BF16)
        for i in range(2):
            top = SUB + (2 * j + i) * 32
            for d in range(NBLK):
                send_ref[d, top : top + 32, :] = part[
                    d * 32 : (d + 1) * 32, i * HEAD : (i + 1) * HEAD
                ]


def out_kernel(hid_ref, w_ref, out_ref):
    out_ref[...] = mm(hid_ref[...], w_ref[...], NN).astype(BF16)


def sum_kernel(parts_ref, gw_ref):
    for half in range(2):
        total = parts_ref[half, SUB:, :].astype(F32)
        for d in range(half + 2, NBLK, 2):
            total = total + parts_ref[d, SUB:, :].astype(F32)
        gw_ref[half * WROWS // 2 : (half + 1) * WROWS // 2, :] = total.astype(BF16)


def add_kernel(*refs):
    parts = [ref[...].astype(F32) for ref in refs[:-1]]
    total = parts[0] + parts[1]
    if len(parts) == 4:
        total = total + (parts[2] + parts[3])
    refs[-1][...] = total.astype(refs[-1].dtype)


def backward_tiles(
    tiles, idx_ref, recv_ref, phik_ref, qp_ref, gate_ref, start_ref, sc_ref, freq_ref, out_ref, top,
    dqp_ref, term_ref,
):
    head, gq, gk = place(idx_ref)
    freq = freq_ref[head].astype(BF16)
    freq = jnp.concatenate([freq, -freq], axis=1)

    def feature_back(phi, grad_phi):
        turned = pltpu.roll(grad_phi, FREQS, 1)
        return mm((phi.astype(F32) * turned).astype(BF16), freq, NT)

    for c in tiles:
        rows = tile_rows(c)
        keys = tile_of(recv_ref, c, K0, V0)
        values = tile_of(recv_ref, c, V0, PACK)
        phik = phik_ref[c * TILE : (c + 1) * TILE, :]
        pairs = diagonal(keys, phik)
        scaled, gate = sc_ref[rows, :], twice(gate_ref[rows, :])
        masked = masker(start_ref, rows, c, gq, gk)
        both = mm(qp_ref[rows, :], pairs, NT)
        half, kern = both[:, :TILE] * (0.5 * SCALE), both[:, TILE:]
        t = jnp.tanh(half)
        weights = half + half * t
        slope = (1.0 + t) + weights * (1.0 - t)
        grad_w = masked(mm(scaled, values, NT))
        both = masked(weights + gate * kern).astype(BF16)
        grad_s = (grad_w * slope * (0.5 * SCALE)).astype(BF16)
        grad_k = (grad_w * gate).astype(BF16)
        term = kern * grad_w
        term_ref[rows, :] += term[:, :HEAD] + term[:, HEAD:]
        dqp_ref[rows, :] += mm(jnp.concatenate([grad_s, grad_k], axis=1), pairs, NN)
        dkey = mm(grad_s, qp_ref[rows, :HEAD], TN)
        dkey = dkey + feature_back(phik, mm(grad_k, qp_ref[rows, HEAD:], TN))
        dval = mm(both, scaled, TN)
        for i in range(SPAN):
            part, b = slice(i * SUB, (i + 1) * SUB), SPAN * c + i
            out_ref[b, top : top + SUB, :] = dkey[part].astype(BF16)
            out_ref[b, top + SUB : top + 2 * SUB, :] = dval[part].astype(BF16)
    return feature_back


def first_backward_kernel(
    idx_ref, recv_ref, phik_ref, qp_ref, gate_ref, start_ref, grads_ref, freq_ref,
    dkv_ref, sc_ref, dqp_ref, term_ref,
):
    for b in range(NBLK):
        sc_ref[b * SUB : (b + 1) * SUB, :] = grads_ref[b, 0:SUB, :]
    dqp_ref[...] = jnp.zeros_like(dqp_ref)
    term_ref[...] = jnp.zeros_like(term_ref)
    backward_tiles(
        range(EARLY), idx_ref, recv_ref, phik_ref, qp_ref, gate_ref, start_ref, sc_ref, freq_ref,
        dkv_ref, 0, dqp_ref, term_ref,
    )


def second_backward_kernel(
    idx_ref, recv_ref, phik_ref, qp_ref, gate_ref, start_ref, sc_ref, dkv_ref, dqp1_ref, term1_ref,
    freq_ref, send_ref, dqp_s, term_s,
):
    dqp_s[...] = dqp1_ref[...]
    term_s[...] = term1_ref[...]
    feature_back = backward_tiles(
        range(EARLY, TILES), idx_ref, recv_ref, phik_ref, qp_ref, gate_ref, start_ref, sc_ref,
        freq_ref, send_ref, K0, dqp_s, term_s,
    )
    for b in range(SPAN * EARLY):
        send_ref[b, K0:PACK, :] = dkv_ref[b]
    dq = dqp_s[:, :HEAD] + feature_back(qp_ref[:, HEAD:], dqp_s[:, HEAD:])
    gate = gate_ref[...]
    term = jnp.sum(term_s[...], axis=1, keepdims=True) * gate * (1.0 - gate) * SCALE
    mine = lanes((SUB, HEAD)) == sublanes((SUB, HEAD))
    for b in range(NBLK):
        rows = slice(b * SUB, (b + 1) * SUB)
        send_ref[b, Q0:G0, :] = dq[rows].astype(BF16)
        across = jnp.sum(jnp.where(mine, term[rows], 0.0), axis=0, keepdims=True)
        send_ref[b, G0:K0, :] = jnp.broadcast_to(across, (16, HEAD)).astype(BF16)


def final_kernel(recv_ref, ghn_ref, gw_ref, dq_ref, dk_ref, dv_ref, dg_ref, dw_ref):
    mine = lanes((SUB, HEAD)) == sublanes((SUB, HEAD))

    def pair(one, two, first, last):
        return recv_ref[one, first:last, :].astype(F32) + recv_ref[two, first:last, :].astype(F32)

    for h in range(HEADS):
        cols = slice(h * HEAD, (h + 1) * HEAD)
        for i in range(2):
            rows = slice(i * SUB, (i + 1) * SUB)
            one, two = device(h, i, 0), device(h, i, 1)
            dq_ref[rows, cols] = pair(one, two, Q0, G0).astype(BF16)
            term = column(pair(one, two, G0, K0)[0:1], mine)
            dg_ref[rows, cols] = (ghn_ref[rows, cols] + term).astype(BF16)
            one, two = device(h, 0, i), device(h, 1, i)
            dk_ref[rows, cols] = pair(one, two, K0, V0).astype(BF16)
            dv_ref[rows, cols] = pair(one, two, V0, PACK).astype(BF16)
    for j in range(D // HEAD):
        dw_ref[:, j * HEAD : (j + 1) * HEAD] = gw_ref[j * 32 : (j + 1) * 32]


VMEM = pl.BlockSpec(memory_space=pltpu.VMEM)
SMEM = pl.BlockSpec(memory_space=pltpu.SMEM)
ANY = pl.BlockSpec(memory_space=pl.ANY)


def call(body, scalars, arrays, outs, scratch=(), us=1.0, space=VMEM, to=VMEM, mib=16, after=(), spaces=None):
    if after:
        inner, first = body, len(scalars) + len(arrays)

        def body(*refs):
            inner(*refs[:first], *refs[first + len(after) :])

    moved = sum(x.size * x.dtype.itemsize for x in arrays)
    moved += sum(math.prod(s) * jnp.dtype(t).itemsize for s, t in outs)
    return pl.pallas_call(
        body,
        in_specs=[SMEM] * len(scalars)
        + (spaces or [space] * len(arrays))
        + [ANY] * len(after),
        out_specs=[to] * len(outs),
        out_shape=[jax.ShapeDtypeStruct(s, t) for s, t in outs],
        scratch_shapes=[pltpu.VMEM(*s) if isinstance(s, tuple) else s for s in scratch],
        compiler_params=pltpu.CompilerParams(vmem_limit_bytes=mib * 1024 * 1024),
        cost_estimate=pl.CostEstimate(
            flops=int(us * 1.1e9), bytes_accessed=moved, transcendentals=0
        ),
    )(*scalars, *arrays, *after)


def swap(a, axis):
    return lax.all_to_all(a, axis, 0, 0, tiled=True)


def cross(x, mask):
    return lax.ppermute(x, "dp", [(i, i ^ mask) for i in range(16)])


def pair(x):
    return lax.ppermute(x, "blk", [(i, i ^ 1) for i in range(NBLK)])


def local(q, k, v, u, freqs, w, lens, cot):
    q, k, v, u, cot, lens = q[0], k[0], v[0], u[0], cot[0], lens
    idx = lax.axis_index("blk").astype(jnp.int32)[None]
    rows, tall = (ROWS, HEAD), (ROWS, 2 * HEAD)
    (send1,) = call(
        pack_kernel,
        [],
        [q, k, v, u],
        [((NBLK, PACK, HEAD), BF16)],
        [((TOK, WIDTH), BF16)] * 4 + [pltpu.SemaphoreType.DMA((4,))],
        space=ANY,
        mib=60,
    )
    recv1 = swap(send1, "blk")
    cot2 = pair(cot)
    (gh,) = call(hidden_grad_kernel, [], [w, cot], [((TOK, WIDTH), F32)])
    mixed, phik, qp, gate, start = call(
        forward_kernel,
        [idx],
        [recv1, freqs, lens],
        [((NBLK, SUB, HEAD), BF16), (rows, BF16), (tall, BF16), (rows, F32), (rows, F32)],
        [(rows, F32), pltpu.SMEM((1, USERS), jnp.int32), pltpu.SemaphoreType.DMA(())],
        spaces=[VMEM, VMEM, ANY],
        after=[gh, cot2],
        us=3.5,
    )
    recv2 = swap(mixed, "blk")
    wide = ((TOK, WIDTH), F32)
    hidden, normed, scales = call(
        norm_kernel,
        [lens, idx],
        [recv2, u],
        [((TOK, WIDTH), BF16), wide, ((TOK, 2 * HEAD), F32)],
        us=0.7,
    )
    hidden2 = pair(hidden)
    scaled, ghn = call(
        scale_kernel, [], [u, gh, normed, scales], [((TOK, WIDTH), BF16), wide], us=0.6
    )
    (send3,) = call(
        weight_kernel,
        [idx],
        [scaled, hidden, hidden2, cot, cot2],
        [((NBLK, SUB + WROWS // 2, HEAD), BF16)],
        us=0.7,
    )
    recv3 = swap(send3, "blk")
    (gw,) = call(sum_kernel, [], [recv3], [((WROWS, HEAD), BF16)])
    (layer_out,) = call(out_kernel, [], [hidden, w], [((TOK, D), BF16)])
    shared = [recv1, phik, qp, gate, start]
    dkv, scaled, dqp, term = call(
        first_backward_kernel,
        [idx],
        shared + [recv3, freqs],
        [((SPAN * EARLY, 2 * SUB, HEAD), BF16), (rows, BF16), (tall, F32), (rows, F32)],
        us=3.0,
    )
    (gw,) = call(
        add_kernel, [], [gw, cross(gw, 8)], [((WROWS, HEAD), BF16)], us=0.5, after=[dkv]
    )
    (send4,) = call(
        second_backward_kernel,
        [idx],
        shared + [scaled, dkv, dqp, term, freqs],
        [((NBLK, PACK, HEAD), BF16)],
        [(tall, F32), (rows, F32)],
        us=3.0,
        after=[gw],
    )
    (gw,) = call(
        add_kernel, [], [gw, cross(gw, 1)], [((WROWS, HEAD), BF16)], us=0.5, after=[send4]
    )
    send4, gw = lax.optimization_barrier((send4, gw))
    parts = [gw] + [cross(gw, mask) for mask in (2, 4, 6)]
    (gw,) = call(add_kernel, [], parts, [((WROWS, HEAD), F32)], us=0.5)
    recv4 = swap(send4, "blk")
    dq, dk, dv, dg, dw = call(
        final_kernel,
        [],
        [recv4, ghn, gw],
        [((TOK, WIDTH), BF16)] * 4 + [((WIDTH // NBLK, D), F32)],
    )
    return layer_out[None], dq[None], dk[None], dv[None], dg[None], dw


def solution(mesh):
    rows = P("dp", "blk", None)
    return jax.shard_map(
        local,
        mesh=mesh,
        in_specs=(rows, rows, rows, rows, P(), P(), P("dp", None), rows),
        out_specs=(rows, rows, rows, rows, rows, P("blk", None)),
        check_vma=False,
    )
```

```python
import math

import jax
import jax.numpy as jnp
from jax import lax
from jax.experimental import pallas as pl
from jax.experimental.pallas import tpu as pltpu
from jax.sharding import PartitionSpec as P

EPS = 1e-05
HEADS, HEAD, FREQS, USERS = 4, 128, 64, 8
TOK, NBLK = 128, 16
SUB = TOK // 2
WIDTH, D = HEADS * HEAD, 1024
ROWS = SUB * NBLK
SPAN = 4
TILE = SPAN * SUB
REACH = 3
TILES = ROWS // TILE
EARLY = 2
SCALE = 1.0 / math.sqrt(HEAD)
F32, BF16 = jnp.float32, jnp.bfloat16

Q0, G0, K0, V0, PACK = 0, SUB, SUB + 16, 2 * SUB + 16, 3 * SUB + 16
WROWS = (WIDTH // NBLK) * D // HEAD


def device(h, gq, gk):
    return 4 * h + 2 * gq + gk


NT = (((1,), (1,)), ((), ()))
NN = (((1,), (0,)), ((), ()))
TN = (((0,), (0,)), ((), ()))


def mm(a, b, dims):
    return lax.dot_general(a, b, dims, preferred_element_type=F32)


def lanes(shape):
    return lax.broadcasted_iota(jnp.int32, shape, 1)


def sublanes(shape):
    return lax.broadcasted_iota(jnp.int32, shape, 0)


def column(row, mine):
    return jnp.sum(jnp.where(mine, row, 0.0), axis=1, keepdims=True)


def starts_of(lens_ref, pos):
    end = jnp.int32(0)
    start = jnp.zeros_like(pos)
    for u in range(USERS):
        end = end + lens_ref[0, u]
        start = jnp.where(pos >= end, end, start)
    return start


def cos_sin(angles):
    turns = jnp.floor(angles * (2.0 / math.pi) + 0.5)
    r = angles - turns * 1.5703125
    r = r - turns * 4.837512969970703125e-4
    r = r - turns * 7.54978995489188e-8
    quad = turns.astype(jnp.int32)
    z = r * r
    c = 1.0 - 0.5 * z + z * z * (4.166664568e-2 + z * (-1.388731625e-3 + z * 2.443315712e-5))
    s = r + r * z * (-1.6666654611e-1 + z * (8.3321608736e-3 - z * 1.9515295891e-4))
    odd = (quad & 1) == 1
    cos, sin = jnp.where(odd, s, c), jnp.where(odd, c, s)
    cos = jnp.where(((quad + 1) & 2) == 2, -cos, cos)
    return cos, jnp.where((quad & 2) == 2, -sin, sin)


def pack_kernel(q_hbm, k_hbm, v_hbm, u_hbm, out_ref, q_ref, k_ref, v_ref, u_ref, sems):
    pairs = ((u_hbm, u_ref), (q_hbm, q_ref), (k_hbm, k_ref), (v_hbm, v_ref))
    copies = [pltpu.make_async_copy(src, dst, sems.at[i]) for i, (src, dst) in enumerate(pairs)]
    for copy in copies:
        copy.start()
    ones = jnp.ones((16, HEAD), BF16)
    copies[0].wait()
    for h in range(HEADS):
        total = mm(ones, u_ref[:, h * HEAD : (h + 1) * HEAD], NT)
        gate = jax.nn.sigmoid(total * SCALE)
        high = gate.astype(BF16).astype(F32)
        gate = jnp.where(sublanes((16, TOK)) < 8, high, gate - high).astype(BF16)
        for d in range(device(h, 0, 0), device(h, 1, 1) + 1):
            out_ref[d, G0:K0, :] = gate
    for copy in copies[1:]:
        copy.wait()
    for h in range(HEADS):
        cols = slice(h * HEAD, (h + 1) * HEAD)
        for gq in range(2):
            for gk in range(2):
                d = device(h, gq, gk)
                out_ref[d, Q0:G0, :] = q_ref[gq * SUB : (gq + 1) * SUB, cols]
                out_ref[d, K0:V0, :] = k_ref[gk * SUB : (gk + 1) * SUB, cols]
                out_ref[d, V0:PACK, :] = v_ref[gk * SUB : (gk + 1) * SUB, cols]


def stage_rows(recv_ref, lens_ref, gq, gate_s, start_s):
    pos = sublanes((NBLK, TOK)) * TOK + lanes((NBLK, TOK))
    starts = starts_of(lens_ref, pos).astype(F32)
    mine = lanes((SUB, TOK)) == sublanes((SUB, TOK)) + gq * SUB
    for b in range(NBLK):
        rows = slice(b * SUB, (b + 1) * SUB)
        parts = recv_ref[b, G0:K0, :].astype(F32)
        gate_s[rows, :] = jnp.broadcast_to(column(parts[0:1] + parts[8:9], mine), (SUB, HEAD))
        start_s[rows, :] = jnp.broadcast_to(column(starts[b : b + 1], mine), (SUB, HEAD))


def tile_of(recv_ref, c, first, last):
    return jnp.concatenate(
        [recv_ref[SPAN * c + i, first:last, :] for i in range(SPAN)], axis=0
    )


def twice(a):
    return jnp.concatenate([a, a], axis=1)


def diagonal(a, b):
    zero = jnp.zeros_like(a)
    return jnp.concatenate(
        [jnp.concatenate([a, zero], axis=1), jnp.concatenate([zero, b], axis=1)], axis=0
    )


def masker(start_s, rows, c, gq, gk):
    lane = lanes((1, TILE))
    key = ((SPAN * c + (lane >> 6)) * TOK + gk * SUB + (lane & (SUB - 1))).astype(F32)
    row = sublanes((TILE, TILE))
    pos = ((SPAN * c + (row >> 6)) * TOK + gq * SUB + (row & (SUB - 1))).astype(F32)
    top = slice(rows.start, rows.start + TILE)
    near = (key >= twice(start_s[top, :])) & (key <= pos)
    if rows.stop == top.stop:
        return lambda x: jnp.where(near, x, 0.0)
    far = key >= twice(start_s[top.stop : rows.stop, :])

    def masked(x):
        return jnp.concatenate(
            [jnp.where(near, x[:TILE], 0.0), jnp.where(far, x[TILE:], 0.0)], axis=0
        )

    return masked


def place(idx_ref):
    return idx_ref[0] // 4, (idx_ref[0] // 2) % 2, idx_ref[0] % 2


def tile_rows(c):
    return slice(c * TILE, min(c + REACH, TILES) * TILE)


def forward_kernel(
    idx_ref, recv_ref, freq_ref, lens_hbm, mixed_ref, phik_ref, qp_ref, gate_ref, start_ref,
    acc_s, lens_s, sem,
):
    copy = pltpu.make_async_copy(lens_hbm, lens_s, sem)
    copy.start()
    head, gq, gk = place(idx_ref)
    freq = freq_ref[head]
    pieces = []
    for _ in range(3):
        piece = freq.astype(BF16)
        pieces.append(diagonal(piece, piece))
        freq = freq - piece.astype(F32)

    def phi_of(x):
        n = x.shape[0] // 2
        x = jnp.concatenate([x[:n], x[n:]], axis=1)
        angles = (mm(x, pieces[2], NN) + mm(x, pieces[1], NN)) + mm(x, pieces[0], NN)
        cos, sin = cos_sin(angles)
        left = lanes((n, HEAD)) < FREQS
        first = jnp.where(left, cos, pltpu.roll(sin, FREQS, 1))
        second = jnp.where(left, pltpu.roll(cos, FREQS, 1), sin)
        return (jnp.concatenate([first, second], axis=0) / math.sqrt(FREQS)).astype(BF16)

    for b in range(NBLK):
        qp_ref[b * SUB : (b + 1) * SUB, :HEAD] = recv_ref[b, Q0:G0, :]
    for i in range(4):
        rows = slice(i * ROWS // 4, (i + 1) * ROWS // 4)
        qp_ref[rows, HEAD:] = phi_of(qp_ref[rows, :HEAD])
    copy.wait()
    stage_rows(recv_ref, lens_s, gq, gate_ref, start_ref)
    acc_s[...] = jnp.zeros_like(acc_s)
    for c in range(TILES):
        rows = tile_rows(c)
        keys = tile_of(recv_ref, c, K0, V0)
        values = tile_of(recv_ref, c, V0, PACK)
        phik = phi_of(keys)
        phik_ref[c * TILE : (c + 1) * TILE, :] = phik
        both = mm(qp_ref[rows, :], diagonal(keys, phik), NT)
        half, kern = both[:, :TILE] * (0.5 * SCALE), both[:, TILE:]
        both = half + half * jnp.tanh(half) + twice(gate_ref[rows, :]) * kern
        both = masker(start_ref, rows, c, gq, gk)(both).astype(BF16)
        acc_s[rows, :] += mm(both, values, NN)
    for b in range(NBLK):
        mixed_ref[b] = acc_s[b * SUB : (b + 1) * SUB, :].astype(BF16)


def hidden_grad_kernel(w_ref, cot_ref, gh_ref):
    gh_ref[...] = mm(cot_ref[...], w_ref[...], NT)


def norm_kernel(lens_ref, idx_ref, mixed_ref, u_ref, hid_ref, normed_ref, scales_ref):
    pos = idx_ref[0] * TOK + sublanes((TOK, HEAD))
    count = (pos - starts_of(lens_ref, pos) + 1).astype(F32)
    inverse = jnp.concatenate([1.0 / count] * HEADS, axis=1)
    mixed = []
    for h in range(HEADS):
        halves = [
            mixed_ref[device(h, gq, 0)].astype(F32) + mixed_ref[device(h, gq, 1)].astype(F32)
            for gq in range(2)
        ]
        mixed.append(jnp.concatenate(halves, axis=0))
    mixed = jnp.concatenate(mixed, axis=1) * inverse
    gates = u_ref[...].astype(F32)
    centered = mixed - jnp.mean(mixed, axis=1, keepdims=True)
    rstd = lax.rsqrt(jnp.mean(centered * centered, axis=1, keepdims=True) + EPS)
    normed = centered * rstd
    hid_ref[...] = (normed * gates).astype(BF16)
    normed_ref[...] = normed
    scales_ref[:, :HEAD] = jnp.broadcast_to(rstd, (TOK, HEAD))
    scales_ref[:, HEAD:] = inverse[:, :HEAD]


def scale_kernel(u_ref, gh_ref, normed_ref, scales_ref, scaled_ref, ghn_ref):
    gates, normed, grad_hidden = u_ref[...].astype(F32), normed_ref[...], gh_ref[...]
    rstd = jnp.concatenate([scales_ref[:, :HEAD]] * HEADS, axis=1)
    inverse = jnp.concatenate([scales_ref[:, HEAD:]] * HEADS, axis=1)
    ghn_ref[...] = grad_hidden * normed
    grad_normed = grad_hidden * gates
    grad_mixed = rstd * (
        grad_normed
        - jnp.mean(grad_normed, axis=1, keepdims=True)
        - normed * jnp.mean(grad_normed * normed, axis=1, keepdims=True)
    )
    scaled_ref[...] = (grad_mixed * inverse).astype(BF16)


def weight_kernel(idx_ref, scaled_ref, hid_ref, hid2_ref, cot_ref, cot2_ref, send_ref):
    for h in range(HEADS):
        for gq in range(2):
            for gk in range(2):
                send_ref[device(h, gq, gk), 0:SUB, :] = scaled_ref[
                    gq * SUB : (gq + 1) * SUB, h * HEAD : (h + 1) * HEAD
                ]
    hidden = jnp.concatenate([hid_ref[...], hid2_ref[...]], axis=0)
    first = (idx_ref[0] % 2) * (D // 2)
    for j in range(D // 2 // 256):
        cols = pl.ds(pl.multiple_of(first + j * 256, 256), 256)
        cots = jnp.concatenate([cot_ref[:, cols], cot2_ref[:, cols]], axis=0)
        part = mm(hidden, cots, TN).astype(BF16)
        for i in range(2):
            top = SUB + (2 * j + i) * 32
            for d in range(NBLK):
                send_ref[d, top : top + 32, :] = part[
                    d * 32 : (d + 1) * 32, i * HEAD : (i + 1) * HEAD
                ]


def out_kernel(hid_ref, w_ref, out_ref):
    out_ref[...] = mm(hid_ref[...], w_ref[...], NN).astype(BF16)


def sum_kernel(parts_ref, gw_ref):
    for half in range(2):
        total = parts_ref[half, SUB:, :].astype(F32)
        for d in range(half + 2, NBLK, 2):
            total = total + parts_ref[d, SUB:, :].astype(F32)
        gw_ref[half * WROWS // 2 : (half + 1) * WROWS // 2, :] = total.astype(BF16)


def add_kernel(*refs):
    parts = [ref[...].astype(F32) for ref in refs[:-1]]
    total = parts[0] + parts[1]
    if len(parts) == 4:
        total = total + (parts[2] + parts[3])
    refs[-1][...] = total.astype(refs[-1].dtype)


def backward_tiles(
    tiles, idx_ref, recv_ref, phik_ref, qp_ref, gate_ref, start_ref, sc_ref, freq_ref, out_ref, top,
    dqp_ref, term_ref,
):
    head, gq, gk = place(idx_ref)
    freq = freq_ref[head].astype(BF16)
    freq = jnp.concatenate([freq, -freq], axis=1)

    def feature_back(phi, grad_phi):
        turned = pltpu.roll(grad_phi, FREQS, 1)
        return mm((phi.astype(F32) * turned).astype(BF16), freq, NT)

    for c in tiles:
        rows = tile_rows(c)
        keys = tile_of(recv_ref, c, K0, V0)
        values = tile_of(recv_ref, c, V0, PACK)
        phik = phik_ref[c * TILE : (c + 1) * TILE, :]
        pairs = diagonal(keys, phik)
        scaled, gate = sc_ref[rows, :], twice(gate_ref[rows, :])
        masked = masker(start_ref, rows, c, gq, gk)
        both = mm(qp_ref[rows, :], pairs, NT)
        half, kern = both[:, :TILE] * (0.5 * SCALE), both[:, TILE:]
        t = jnp.tanh(half)
        weights = half + half * t
        slope = (1.0 + t) + weights * (1.0 - t)
        grad_w = masked(mm(scaled, values, NT))
        both = masked(weights + gate * kern).astype(BF16)
        grad_s = (grad_w * slope * (0.5 * SCALE)).astype(BF16)
        grad_k = (grad_w * gate).astype(BF16)
        term = kern * grad_w
        term_ref[rows, :] += term[:, :HEAD] + term[:, HEAD:]
        dqp_ref[rows, :] += mm(jnp.concatenate([grad_s, grad_k], axis=1), pairs, NN)
        dkey = mm(grad_s, qp_ref[rows, :HEAD], TN)
        dkey = dkey + feature_back(phik, mm(grad_k, qp_ref[rows, HEAD:], TN))
        dval = mm(both, scaled, TN)
        for i in range(SPAN):
            part, b = slice(i * SUB, (i + 1) * SUB), SPAN * c + i
            out_ref[b, top : top + SUB, :] = dkey[part].astype(BF16)
            out_ref[b, top + SUB : top + 2 * SUB, :] = dval[part].astype(BF16)
    return feature_back


def first_backward_kernel(
    idx_ref, recv_ref, phik_ref, qp_ref, gate_ref, start_ref, grads_ref, freq_ref,
    dkv_ref, sc_ref, dqp_ref, term_ref,
):
    for b in range(NBLK):
        sc_ref[b * SUB : (b + 1) * SUB, :] = grads_ref[b, 0:SUB, :]
    dqp_ref[...] = jnp.zeros_like(dqp_ref)
    term_ref[...] = jnp.zeros_like(term_ref)
    backward_tiles(
        range(EARLY), idx_ref, recv_ref, phik_ref, qp_ref, gate_ref, start_ref, sc_ref, freq_ref,
        dkv_ref, 0, dqp_ref, term_ref,
    )


def second_backward_kernel(
    idx_ref, recv_ref, phik_ref, qp_ref, gate_ref, start_ref, sc_ref, dkv_ref, dqp1_ref, term1_ref,
    freq_ref, send_ref, dqp_s, term_s,
):
    dqp_s[...] = dqp1_ref[...]
    term_s[...] = term1_ref[...]
    feature_back = backward_tiles(
        range(EARLY, TILES), idx_ref, recv_ref, phik_ref, qp_ref, gate_ref, start_ref, sc_ref,
        freq_ref, send_ref, K0, dqp_s, term_s,
    )
    for b in range(SPAN * EARLY):
        send_ref[b, K0:PACK, :] = dkv_ref[b]
    dq = dqp_s[:, :HEAD] + feature_back(qp_ref[:, HEAD:], dqp_s[:, HEAD:])
    gate = gate_ref[...]
    term = jnp.sum(term_s[...], axis=1, keepdims=True) * gate * (1.0 - gate) * SCALE
    mine = lanes((SUB, HEAD)) == sublanes((SUB, HEAD))
    for b in range(NBLK):
        rows = slice(b * SUB, (b + 1) * SUB)
        send_ref[b, Q0:G0, :] = dq[rows].astype(BF16)
        across = jnp.sum(jnp.where(mine, term[rows], 0.0), axis=0, keepdims=True)
        send_ref[b, G0:K0, :] = jnp.broadcast_to(across, (16, HEAD)).astype(BF16)


def final_kernel(recv_ref, ghn_ref, gw_ref, dq_ref, dk_ref, dv_ref, dg_ref, dw_ref):
    mine = lanes((SUB, HEAD)) == sublanes((SUB, HEAD))

    def pair(one, two, first, last):
        return recv_ref[one, first:last, :].astype(F32) + recv_ref[two, first:last, :].astype(F32)

    for h in range(HEADS):
        cols = slice(h * HEAD, (h + 1) * HEAD)
        for i in range(2):
            rows = slice(i * SUB, (i + 1) * SUB)
            one, two = device(h, i, 0), device(h, i, 1)
            dq_ref[rows, cols] = pair(one, two, Q0, G0).astype(BF16)
            term = column(pair(one, two, G0, K0)[0:1], mine)
            dg_ref[rows, cols] = (ghn_ref[rows, cols] + term).astype(BF16)
            one, two = device(h, 0, i), device(h, 1, i)
            dk_ref[rows, cols] = pair(one, two, K0, V0).astype(BF16)
            dv_ref[rows, cols] = pair(one, two, V0, PACK).astype(BF16)
    for j in range(D // HEAD):
        dw_ref[:, j * HEAD : (j + 1) * HEAD] = gw_ref[j * 32 : (j + 1) * 32]


VMEM = pl.BlockSpec(memory_space=pltpu.VMEM)
SMEM = pl.BlockSpec(memory_space=pltpu.SMEM)
ANY = pl.BlockSpec(memory_space=pl.ANY)


def call(body, scalars, arrays, outs, scratch=(), us=1.0, space=VMEM, to=VMEM, mib=16, after=(), spaces=None):
    if after:
        inner, first = body, len(scalars) + len(arrays)

        def body(*refs):
            inner(*refs[:first], *refs[first + len(after) :])

    moved = sum(x.size * x.dtype.itemsize for x in arrays)
    moved += sum(math.prod(s) * jnp.dtype(t).itemsize for s, t in outs)
    return pl.pallas_call(
        body,
        in_specs=[SMEM] * len(scalars)
        + (spaces or [space] * len(arrays))
        + [ANY] * len(after),
        out_specs=[to] * len(outs),
        out_shape=[jax.ShapeDtypeStruct(s, t) for s, t in outs],
        scratch_shapes=[pltpu.VMEM(*s) if isinstance(s, tuple) else s for s in scratch],
        compiler_params=pltpu.CompilerParams(vmem_limit_bytes=mib * 1024 * 1024),
        cost_estimate=pl.CostEstimate(
            flops=int(us * 1.1e9), bytes_accessed=moved, transcendentals=0
        ),
    )(*scalars, *arrays, *after)


def swap(a, axis):
    return lax.all_to_all(a, axis, 0, 0, tiled=True)


def cross(x, mask):
    return lax.ppermute(x, "dp", [(i, i ^ mask) for i in range(16)])


def pair(x):
    return lax.ppermute(x, "blk", [(i, i ^ 1) for i in range(NBLK)])


def local(q, k, v, u, freqs, w, lens, cot):
    q, k, v, u, cot, lens = q[0], k[0], v[0], u[0], cot[0], lens
    idx = lax.axis_index("blk").astype(jnp.int32)[None]
    rows, tall = (ROWS, HEAD), (ROWS, 2 * HEAD)
    (send1,) = call(
        pack_kernel,
        [],
        [q, k, v, u],
        [((NBLK, PACK, HEAD), BF16)],
        [((TOK, WIDTH), BF16)] * 4 + [pltpu.SemaphoreType.DMA((4,))],
        space=ANY,
        mib=60,
    )
    recv1 = swap(send1, "blk")
    cot2 = pair(cot)
    (gh,) = call(hidden_grad_kernel, [], [w, cot], [((TOK, WIDTH), F32)])
    mixed, phik, qp, gate, start = call(
        forward_kernel,
        [idx],
        [recv1, freqs, lens],
        [((NBLK, SUB, HEAD), BF16), (rows, BF16), (tall, BF16), (rows, F32), (rows, F32)],
        [(rows, F32), pltpu.SMEM((1, USERS), jnp.int32), pltpu.SemaphoreType.DMA(())],
        spaces=[VMEM, VMEM, ANY],
        after=[gh, cot2],
        us=3.5,
    )
    recv2 = swap(mixed, "blk")
    wide = ((TOK, WIDTH), F32)
    hidden, normed, scales = call(
        norm_kernel,
        [lens, idx],
        [recv2, u],
        [((TOK, WIDTH), BF16), wide, ((TOK, 2 * HEAD), F32)],
        us=0.7,
    )
    hidden2 = pair(hidden)
    scaled, ghn = call(
        scale_kernel, [], [u, gh, normed, scales], [((TOK, WIDTH), BF16), wide], us=0.6
    )
    (send3,) = call(
        weight_kernel,
        [idx],
        [scaled, hidden, hidden2, cot, cot2],
        [((NBLK, SUB + WROWS // 2, HEAD), BF16)],
        us=0.7,
    )
    recv3 = swap(send3, "blk")
    (gw,) = call(sum_kernel, [], [recv3], [((WROWS, HEAD), BF16)])
    (layer_out,) = call(out_kernel, [], [hidden, w], [((TOK, D), BF16)])
    shared = [recv1, phik, qp, gate, start]
    dkv, scaled, dqp, term = call(
        first_backward_kernel,
        [idx],
        shared + [recv3, freqs],
        [((SPAN * EARLY, 2 * SUB, HEAD), BF16), (rows, BF16), (tall, F32), (rows, F32)],
        us=3.0,
    )
    (gw,) = call(
        add_kernel, [], [gw, cross(gw, 8)], [((WROWS, HEAD), BF16)], us=0.5, after=[dkv]
    )
    (send4,) = call(
        second_backward_kernel,
        [idx],
        shared + [scaled, dkv, dqp, term, freqs],
        [((NBLK, PACK, HEAD), BF16)],
        [(tall, F32), (rows, F32)],
        us=3.0,
        after=[gw],
    )
    other = cross(gw, 1)
    send4, other = lax.optimization_barrier((send4, other))
    (gw,) = call(add_kernel, [], [gw, other], [((WROWS, HEAD), BF16)], us=0.5)
    parts = [gw] + [cross(gw, mask) for mask in (2, 4, 6)]
    (gw,) = call(add_kernel, [], parts, [((WROWS, HEAD), F32)], us=0.5)
    recv4 = swap(send4, "blk")
    dq, dk, dv, dg, dw = call(
        final_kernel,
        [],
        [recv4, ghn, gw],
        [((TOK, WIDTH), BF16)] * 4 + [((WIDTH // NBLK, D), F32)],
    )
    return layer_out[None], dq[None], dk[None], dv[None], dg[None], dw


def solution(mesh):
    rows = P("dp", "blk", None)
    return jax.shard_map(
        local,
        mesh=mesh,
        in_specs=(rows, rows, rows, rows, P(), P(), P("dp", None), rows),
        out_specs=(rows, rows, rows, rows, rows, P("blk", None)),
        check_vma=False,
    )
```
